256 devices in a mesh: ctx: 64 (over x, z, core), head: 4 (over y).
Axes of the slice: x: 4, y: 4, z: 8, core: 2. Of those that a mesh axis runs over, the one named last changes fastest.
Arguments:
- feat_in: bfloat16 [16384, 8192], P('ctx', 'head'), may hold values from -6 to 6
- gate_in: bfloat16 [16384, 8192], P('ctx', 'head'), may hold values from -6 to 6
- state_proj: bfloat16 [16384, 256], P('ctx'), may hold values from -1.5 to 1.5
- step_raw: float32 [64, 16384], P('head', 'ctx'), may hold values from -6 to 6
- doc_offset: int32 [16384], P('ctx'), may hold values from 0 to 4095, as said below
- feat_taps: float32 [4, 8192], P(None, 'head'), may hold values from -3 to 3
- feat_bias: float32 [8192], P('head'), may hold values from -1.5 to 1.5
- proj_taps: float32 [4, 256], replicated, may hold values from -3 to 3
- proj_bias: float32 [256], replicated, may hold values from -0.6 to 0.6
- step_bias: float32 [64], P('head'), may hold values from -4 to -1
- decay_log: float32 [64], P('head'), may hold values from -13 to -0.7
- skip_gain: float32 [64], P('head'), may hold values from 0.5 to 1.5
- norm_gain: float32 [8192], P('head'), may hold values from 0.1 to 1.9
Outputs:
- mixer_out: bfloat16 [16384, 8192], P('ctx', 'head')
The draws below stay inside these ranges and needn't reach their ends.
Inputs may be any that keep to these rules, and one draw needn't show every extreme that they name: `doc_offset`: the position of each token within its document: 0 at a document's first token, rising by one per token inside it. A document holds at most 4096 tokens, and every document but the window's last holds more than 512.
All inputs are finite; a program needn't handle non-finite values.
Results may differ from the reference program's by a relative error of at most 0.006.
Values may be sent and summed in bfloat16 or wider, within the bound.
No kernel may reach another device: no remote copies, remote signals or barrier semaphores. Data moves between devices by JAX's collectives and lax.ppermute only.
A program may use at most 64 MiB of HBM per device.

```python
import jax
import jax.numpy as jnp
from jax import lax

HEADS = 64
HEAD_DIM = 128
STATE = 128
CONV = 4
BLK = 256
TOKENS = 16384
DOCMAX = 4096


def draw_doc_offset(key, part):
    base_key = jax.random.fold_in(key, 17)
    key_lengths, key_choice = jax.random.split(base_key)
    doc_count = 8 * TOKENS // DOCMAX + 4
    lengths = jax.random.randint(key_lengths, (doc_count,), DOCMAX // 8 + 1, DOCMAX + 1, dtype=jnp.int32)
    chosen = jax.random.randint(key_choice, (), 0, 4, dtype=jnp.int32)
    doc_index = jnp.arange(doc_count, dtype=jnp.int32)
    lengths = jnp.where(doc_index == chosen, DOCMAX, lengths)
    starts = (jnp.cumsum(lengths) - lengths).astype(jnp.int32)
    places = jnp.arange(TOKENS, dtype=jnp.int32)
    owners = (jnp.searchsorted(starts, places, side='right') - 1).astype(jnp.int32)
    return (places - starts[owners]).astype(jnp.int32)


def block_levels(stream_key, shape, cuts, smallest, top_value):
    def one(dim, blocks):
        heights = jax.random.uniform(jax.random.fold_in(jax.random.fold_in(stream_key, 6), dim), (blocks,), jnp.float32, smallest / len(cuts), top_value / len(cuts))
        return jnp.repeat(jnp.exp(heights), shape[dim] // blocks).reshape((-1,) + (1,) * (len(shape) - dim - 1))

    level = one(*cuts[0])
    for cut in cuts[1:]:
        level = level * one(*cut)
    return level


def bell_draw(rng, dims, scale, limit, cuts=(), kind=jnp.bfloat16):
    result = scale * jax.random.normal(rng, dims, jnp.float32)
    if cuts:
        result = result * block_levels(rng, dims, cuts, -0.22, 0.18)
    return jnp.clip(result, -limit, limit).astype(kind)


def setup_inputs(seed: int = 0) -> dict:
    arg_keys = jax.random.split(jax.random.key(seed), 14)
    return {
        "feat_in": bell_draw(arg_keys[0], (TOKENS, HEADS * HEAD_DIM), 1.0, 6.0, ((0, 64), (1, 4))),
        "gate_in": bell_draw(arg_keys[1], (TOKENS, HEADS * HEAD_DIM), 1.0, 6.0, ((0, 64), (1, 4))),
        "state_proj": bell_draw(arg_keys[2], (TOKENS, 2 * STATE), 0.25, 1.5, ((0, 64),)),
        "step_raw": bell_draw(arg_keys[3], (HEADS, TOKENS), 1.0, 6.0, ((0, 4), (1, 64)), jnp.float32),
        "doc_offset": draw_doc_offset(jax.random.fold_in(arg_keys[13], 71), 0),
        "feat_taps": bell_draw(arg_keys[5], (CONV, HEADS * HEAD_DIM), 0.5, 3.0, ((1, 4),), jnp.float32),
        "feat_bias": bell_draw(arg_keys[6], (HEADS * HEAD_DIM,), 0.25, 1.5, ((0, 4),), jnp.float32),
        "proj_taps": bell_draw(arg_keys[7], (CONV, 2 * STATE), 0.5, 3.0, (), jnp.float32),
        "proj_bias": bell_draw(arg_keys[8], (2 * STATE,), 0.1, 0.6, (), jnp.float32),
        "step_bias": jnp.clip(-4.0 + 3.0 * jax.random.uniform(arg_keys[9], (HEADS,), jnp.float32) ** block_levels(arg_keys[9], (HEADS,), ((0, 4),), -0.2, 0.2), -4.0, -1.0),
        "decay_log": jnp.clip(-13.0 + 12.3 * jax.random.uniform(arg_keys[10], (HEADS,), jnp.float32) ** block_levels(arg_keys[10], (HEADS,), ((0, 4),), -0.2, 0.2), -13.0, -0.7),
        "skip_gain": jnp.clip(0.5 + 1.0 * jax.random.uniform(arg_keys[11], (HEADS,), jnp.float32) ** block_levels(arg_keys[11], (HEADS,), ((0, 4),), -0.2, 0.2), 0.5, 1.5),
        "norm_gain": jnp.clip(1.0 + 0.18 * jax.random.normal(arg_keys[12], (HEADS * HEAD_DIM,), jnp.float32), 0.1, 1.9),
    }


def conv_silu(values, kernel_taps, kernel_bias, offsets):
    row_count = values.shape[0]
    tap_count = kernel_taps.shape[0]
    widened = values.astype(jnp.float32)
    summed = jnp.broadcast_to(kernel_bias[None, :], values.shape).astype(jnp.float32)
    for tap_index in range(tap_count):
        tap_lag = tap_count - 1 - tap_index
        shifted = jnp.pad(widened, ((tap_lag, 0), (0, 0)))[:row_count]
        summed = summed + jnp.where((offsets >= tap_lag)[:, None], kernel_taps[tap_index][None, :] * shifted, 0.0)
    return jax.nn.silu(summed).astype(jnp.bfloat16)

def reference(feat_in, gate_in, state_proj, step_raw, doc_offset, feat_taps, feat_bias, proj_taps, proj_bias, step_bias, decay_log, skip_gain, norm_gain):
    conv_proj = conv_silu(state_proj, proj_taps, proj_bias, doc_offset)
    blocks = TOKENS // BLK
    in_proj = conv_proj[:, :STATE].reshape(blocks, BLK, STATE)
    out_proj = conv_proj[:, STATE:].reshape(blocks, BLK, STATE)
    offsets = doc_offset.reshape(blocks, BLK)
    position = jnp.arange(BLK, dtype=jnp.int32)
    causal = position[None, :] <= position[:, None]
    final_row = BLK - 1

    def gated_head(head_index):
        column = (head_index * HEAD_DIM).astype(jnp.int32)
        feat_cols = lax.dynamic_slice_in_dim(feat_in, column, HEAD_DIM, 1)
        taps_cols = lax.dynamic_slice_in_dim(feat_taps, column, HEAD_DIM, 1)
        bias_cols = lax.dynamic_slice_in_dim(feat_bias, column, HEAD_DIM, 0)
        conv_feat = conv_silu(feat_cols, taps_cols, bias_cols, doc_offset)
        raw_row = lax.dynamic_index_in_dim(step_raw, head_index, 0, keepdims=False)
        step_row = jax.nn.softplus(raw_row + step_bias[head_index])
        rate_row = step_row * -jnp.exp(decay_log[head_index])
        skip_value = skip_gain[head_index]

        def one_block(state_in, pieces):
            feat_block, in_block, out_block, rate_block, step_block, offset_block = pieces
            cumulative = jnp.cumsum(rate_block)
            same_doc = causal & (offset_block[:, None] >= position[:, None] - position[None, :])
            scores = jnp.dot(out_block, in_block.T, preferred_element_type=jnp.float32)
            exponent_gap = jnp.where(same_doc, cumulative[:, None] - cumulative[None, :], -jnp.inf)
            weights = (scores * jnp.exp(exponent_gap) * step_block[None, :]).astype(jnp.bfloat16)
            inner_out = jnp.dot(weights, feat_block, preferred_element_type=jnp.float32)
            reaches = offset_block >= position + 1
            lift_factor = jnp.where(reaches, jnp.exp(cumulative), 0.0)
            from_state = jnp.dot(out_block.astype(jnp.float32), state_in.T, precision=lax.Precision.HIGHEST) * lift_factor[:, None]
            ssm_out = inner_out + from_state + skip_value * feat_block.astype(jnp.float32)
            tail_mask = offset_block[final_row] >= final_row - position
            tail_coef = jnp.where(tail_mask, jnp.exp(cumulative[final_row] - cumulative) * step_block, 0.0)
            scaled = (in_block.astype(jnp.float32) * tail_coef[:, None]).astype(jnp.bfloat16)
            contrib = jnp.dot(feat_block.T, scaled, preferred_element_type=jnp.float32)
            keep_factor = jnp.where(reaches[final_row], jnp.exp(cumulative[final_row]), 0.0)
            return (keep_factor * state_in + contrib, ssm_out)
        pieces = (conv_feat.reshape(blocks, BLK, HEAD_DIM), in_proj, out_proj, rate_row.reshape(blocks, BLK), step_row.reshape(blocks, BLK), offsets)
        scanned = lax.scan(one_block, jnp.zeros((HEAD_DIM, STATE), jnp.float32), pieces)
        gate_cols = lax.dynamic_slice_in_dim(gate_in, column, HEAD_DIM, 1).astype(jnp.float32)
        return scanned[1].reshape(TOKENS, HEAD_DIM) * jax.nn.silu(gate_cols)

    def add_squares(carried, head_index):
        gated = gated_head(head_index)
        return (carried + lax.optimization_barrier(jnp.sum(gated * gated, axis=1)), None)
    summed = lax.scan(add_squares, jnp.zeros((TOKENS,), jnp.float32), jnp.arange(HEADS, dtype=jnp.int32))
    scale = lax.rsqrt(summed[0] / (HEADS * HEAD_DIM) + 1e-05)

    def finish(head_index):
        gated = gated_head(head_index)
        gain_cols = lax.dynamic_slice_in_dim(norm_gain, (head_index * HEAD_DIM).astype(jnp.int32), HEAD_DIM, 0)
        return (gated * scale[:, None] * gain_cols[None, :]).astype(jnp.bfloat16)
    normed = lax.map(finish, jnp.arange(HEADS, dtype=jnp.int32))
    return jnp.transpose(normed, (1, 0, 2)).reshape(TOKENS, HEADS * HEAD_DIM)
```

```python
import functools

import jax
import jax.numpy as jnp
from jax import lax
from jax.experimental import pallas as pl
from jax.experimental.pallas import tpu as pltpu
from jax.sharding import PartitionSpec as P

F32 = jnp.float32
BF16 = jnp.bfloat16
ROWS = 256
HEADS = 16
HALF = 8
HD = 128
COLS = HEADS * HD
TAPS = 4
XS, ZS, CS, YS = 4, 8, 2, 4
LOG2E = 1.4426950408889634
VMEM_LIMIT = 40 * 1024 * 1024


def spots():
    return [(x, z, c) for x in range(XS) for z in range(ZS) for c in range(CS)]


def place(x, z, c):
    return (x * ZS + z) * CS + c


def route(to):
    pairs = []
    for x, z, c in spots():
        target = to(x, z, c)
        if target is not None:
            pairs.append((place(x, z, c), place(*target)))
    return pairs


NEXT = [(i, i + 1) for i in range(XS * ZS * CS - 1)]
CORE = route(lambda x, z, c: (x, z, 1 - c))


APART = route(lambda x, z, c: (x, z ^ (1 + 2 * c), c))
TWO = route(lambda x, z, c: (x, z ^ 2, c))


def to_later_group(x, z, c):
    if c == 0 and z < 4:
        return (x, z ^ 6, c)
    if x + 1 == XS:
        return None
    return (x + 1, z ^ 6 if c == 0 else z, c)


LATER = route(to_later_group)
HEAD_XOR = {m: [(i, i ^ m) for i in range(YS)] for m in (1, 2, 3)}


def my_core():
    return lax.rem(lax.axis_index("ctx"), 2)


def my_spot():
    return lax.rem(lax.div(lax.axis_index("ctx"), 2), 4)


def my_slice():
    z = lax.rem(lax.div(lax.axis_index("ctx"), 2), ZS)
    spot = lax.rem(z, 4)
    return jnp.where(z >= 4, lax.bitwise_xor(spot, 2), spot)


def silu(v):
    half = 0.5 * v
    return half + half * jnp.tanh(half)


def conv_rows(xs, taps_ref, bias_ref, cols, scratch_cols, base, rows, masks):
    acc = jnp.broadcast_to(bias_ref[0:1, cols], (rows, HD))
    for k in range(TAPS):
        lag = TAPS - 1 - k
        window = xs[base - lag : base - lag + rows, scratch_cols]
        if lag:
            window = jnp.where(masks[lag], window, 0.0)
        acc = acc + taps_ref[k : k + 1, cols] * window
    return silu(acc).astype(BF16)


PACK = 640
PACKS = [(j, min(PACK, COLS + 256 - j)) for j in range(0, COLS + 256, PACK)]


def edge_kernel(
    doc_hbm, feat_hbm, proj_hbm, ftaps_hbm, fbias_hbm, ptaps_hbm, pbias_hbm, raw_hbm,
    out_ref, docv_ref, feat_ref, proj_ref, ftaps_ref, fbias_ref, ptaps_ref, pbias_ref, raw_ref,
    doc_ref, sems,
):
    copies = [
        pltpu.make_async_copy(source, target, sems.at[n])
        for n, (source, target) in enumerate((
            (feat_hbm, feat_ref), (proj_hbm, proj_ref), (doc_hbm, doc_ref),
            (ftaps_hbm, ftaps_ref), (fbias_hbm, fbias_ref), (ptaps_hbm, ptaps_ref),
            (pbias_hbm, pbias_ref), (raw_hbm, raw_ref),
        ))
    ]
    for copy in copies:
        copy.start()
    for copy in copies[:2]:
        copy.wait()
    last = jnp.concatenate(
        [feat_ref[ROWS - 16 :, :].astype(F32), proj_ref[ROWS - 16 :, :].astype(F32)], axis=1
    )
    last = last[16 - (TAPS - 1) :]
    rows = []
    for j, width in PACKS:
        piece = last[:, j : j + width]
        if width < PACK:
            piece = jnp.concatenate([piece, jnp.zeros((TAPS - 1, PACK - width), F32)], axis=1)
        rows.append(piece)
    rows.append(jnp.zeros((16 - (TAPS - 1) * len(PACKS), PACK), F32))
    out_ref[...] = jnp.concatenate(rows, axis=0).astype(BF16)
    for copy in copies[2:]:
        copy.wait()
    row = lax.broadcasted_iota(jnp.int32, (8, HD), 0)
    docv_ref[...] = jnp.where(row == 0, doc_ref[0], (ROWS - 1) - doc_ref[ROWS - 1])


def split_decay(value):
    high = jnp.floor(value * 256.0) * (1.0 / 256.0)
    return jnp.concatenate([high, value - high], axis=0).astype(BF16)


def joined_decay(tile):
    wide = tile.astype(F32)
    half = tile.shape[0] // 2
    return wide[:half] + wide[half:]


def conv_kernel(
    docv_ref, feat_ref, proj_ref, ftaps_ref, fbias_ref, ptaps_ref, pbias_ref, raw_ref,
    sbias_hbm, dlog_hbm,
    featc_ref, projc_ref, cum_ref, step_ref, coef_ref, decay_ref, sbias_ref, dlog_ref, sems,
):
    copies = [
        pltpu.make_async_copy(sbias_hbm, sbias_ref, sems.at[0]),
        pltpu.make_async_copy(dlog_hbm, dlog_ref, sems.at[1]),
    ]
    for copy in copies:
        copy.start()
    first, start = docv_ref[0:1], docv_ref[1:2]
    first = jnp.concatenate([first, first], axis=1)
    start = jnp.concatenate([start, start], axis=1)
    t = lax.broadcasted_iota(jnp.int32, (ROWS, ROWS), 0)
    s = lax.broadcasted_iota(jnp.int32, (ROWS, ROWS), 1)
    offs = jnp.where((start > 0) & (t >= start), t - start, first + t)
    shifts = [
        jnp.where((t - s == lag) & (offs >= lag), 1.0, 0.0).astype(BF16) for lag in (1, 2, 3)
    ]

    def conv(x_ref, taps_ref, bias_ref, out_ref):
        for j in range(0, out_ref.shape[1], 256):
            cols = slice(j, j + 256)
            x = x_ref[:, cols]
            acc = jnp.broadcast_to(bias_ref[0:1, cols], (ROWS, 256))
            for k in range(TAPS):
                lag = TAPS - 1 - k
                if lag:
                    moved = jnp.dot(shifts[lag - 1], x, preferred_element_type=F32)
                else:
                    moved = x.astype(F32)
                acc = acc + taps_ref[k : k + 1, cols] * moved
            out_ref[:, cols] = silu(acc).astype(BF16)

    conv(proj_ref, ptaps_ref, pbias_ref, projc_ref)
    conv(feat_ref, ftaps_ref, fbias_ref, featc_ref)

    for copy in copies:
        copy.wait()
    first, start = first[:, 0:1], start[:, 0:1]
    line = lax.broadcasted_iota(jnp.int32, (HEADS, ROWS), 0)
    lane = lax.broadcasted_iota(jnp.int32, (HEADS, ROWS), 1)
    bias = jnp.zeros((HEADS, ROWS), F32)
    speed = jnp.zeros((HEADS, ROWS), F32)
    for h in range(HEADS):
        bias = jnp.where(line == h, sbias_ref[h], bias)
        speed = jnp.where(line == h, dlog_ref[h], speed)
    v = raw_ref[...] + bias
    step = jnp.maximum(v, 0.0) + jnp.log1p(jnp.exp(-jnp.abs(v)))
    cum = -step * jnp.exp(speed)
    shift = 1
    while shift < ROWS:
        cum = cum + jnp.where(lane >= shift, pltpu.roll(cum, shift, 1), 0.0)
        shift *= 2
    last = cum[:, ROWS - 1 : ROWS]
    cum_ref[...] = cum
    step_ref[...] = step
    tail = (start <= 0) | (lane >= start)
    coef_ref[...] = jnp.where(tail, jnp.exp(last - cum) * step, 0.0)
    kept = (docv_ref[1:2] < 0) & (docv_ref[0:1] >= 1)
    decay_ref[...] = jnp.where(kept, jnp.broadcast_to(jnp.exp(last), (HEADS, HD)), 0.0)


def state_kernel(
    docv_ref, rim_ref, feat_ref, proj_ref, ftaps_ref, fbias_ref, ptaps_ref, pbias_ref,
    coef_ref, decay_ref, featc_in, projc_in,
    featc_ref, projc_ref, keep_ref, send_ref, xs,
):
    del featc_in, projc_in
    rim = rim_ref[...].astype(F32)
    for n, (j, width) in enumerate(PACKS):
        xs[16 - (TAPS - 1) : 16, j : j + width] = rim[
            n * (TAPS - 1) : (n + 1) * (TAPS - 1), :width
        ]
    xs[16:32, :COLS] = feat_ref[0:16, :].astype(F32)
    xs[16:32, COLS:] = proj_ref[0:16, :].astype(F32)
    first, start = docv_ref[0:1], docv_ref[1:2]
    t = lax.broadcasted_iota(jnp.int32, (16, HD), 0)
    offs = jnp.where((start > 0) & (t >= start), t - start, first + t)
    masks = {lag: offs >= lag for lag in (1, 2, 3)}
    for j in range(2):
        cols = slice(j * HD, (j + 1) * HD)
        there = slice(COLS + j * HD, COLS + (j + 1) * HD)
        projc_ref[0:16, cols] = conv_rows(xs, ptaps_ref, pbias_ref, cols, there, 16, 16, masks)
    for j in range(HEADS):
        cols = slice(j * HD, (j + 1) * HD)
        featc_ref[0:16, cols] = conv_rows(xs, ftaps_ref, fbias_ref, cols, cols, 16, 16, masks)
    turned = projc_ref[:, :HD].astype(F32).T
    for h in range(HEADS):
        rows = slice(h * HD, (h + 1) * HD)
        scaled = (turned * coef_ref[h : h + 1, :]).astype(BF16)
        added = jnp.dot(scaled, featc_ref[:, rows], preferred_element_type=F32)
        keep_ref[rows, :] = added
        send_ref[rows, :] = added.astype(BF16)
    send_ref[COLS:, :] = split_decay(decay_ref[...])


def chip_kernel(keep_ref, decay_ref, recv_ref, own_ref, own_decay_ref, a_ref, b_ref, decays):
    core = my_core()
    second = core == 1
    k = my_slice()
    theirs = joined_decay(recv_ref[COLS:, :])
    mine = decay_ref[...]
    decays[0:16, :] = jnp.where(second, mine, theirs)
    decays[16:32, :] = mine * theirs
    decays[32:40, :] = jnp.zeros((8, HD), F32)

    def combined(h):
        rows = pl.ds(pl.multiple_of(h * HD, HD), HD)
        a = keep_ref[rows, :]
        b = recv_ref[rows, :].astype(F32)
        return decays[pl.ds(h, 1), :] * jnp.where(second, b, a) + jnp.where(second, a, b)

    s = lax.bitwise_xor(k, 1 + 2 * core)
    for i in range(4):
        a_ref[i * HD : (i + 1) * HD, :] = combined(4 * s + i).astype(BF16)
    a_ref[4 * HD :, :] = split_decay(decays[pl.ds(16 + 4 * s, 8), :])
    s = lax.bitwise_xor(k, 2)
    for i in range(2):
        b_ref[i * HD : (i + 1) * HD, :] = combined(4 * s + 2 * core + i).astype(BF16)
    b_ref[2 * HD :, :] = split_decay(decays[pl.ds(16 + 4 * s, 8), :])
    for i in range(4):
        own_ref[i * HD : (i + 1) * HD, :] = combined(4 * k + i)
    own_decay_ref[...] = decays[pl.ds(16 + 4 * k, 8), :]


QUARTER = 4 * HD


def half_rows(core):
    return pl.ds(pl.multiple_of(core * 2 * HD, 2 * HD), 2 * HD)


def group_kernel(
    own_ref, own_decay_ref, ra_ref, ga_ref, rb_ref, gb_ref,
    total_ref, chips_ref, decays_ref,
):
    core = my_core()
    spot = my_spot()
    chips_ref[spot] = own_ref[...]
    decays_ref[spot] = own_decay_ref[...]
    for ref, m in ((ra_ref, 1 + 2 * core), (ga_ref, 3 - 2 * core)):
        there = lax.bitwise_xor(spot, m)
        chips_ref[there] = ref[:QUARTER, :].astype(F32)
        decays_ref[there] = joined_decay(ref[QUARTER:, :])
    there = lax.bitwise_xor(spot, 2)
    chips_ref[there, half_rows(core), :] = rb_ref[: 2 * HD, :].astype(F32)
    chips_ref[there, half_rows(1 - core), :] = gb_ref[: 2 * HD, :].astype(F32)
    decays_ref[there] = joined_decay(rb_ref[2 * HD :, :])
    for i in range(4):
        rows = slice(i * HD, (i + 1) * HD)
        total = chips_ref[0, rows, :]
        for q in range(1, 4):
            total = decays_ref[q, i : i + 1, :] * total + chips_ref[q, rows, :]
        total_ref[rows, :] = total.astype(BF16)
    total_ref[QUARTER:, :] = split_decay(
        decays_ref[0] * decays_ref[1] * decays_ref[2] * decays_ref[3]
    )


def enter_kernel(chips_ref, decays_ref, q_ref, other_ref, own_ref, a_ref, b_ref, states):
    core = my_core()
    second = core == 1
    spot = my_spot()
    q = q_ref[...].astype(F32)
    other = other_ref[...].astype(F32)
    before = jnp.where(second, other, q)
    farther = jnp.where(second, q, other)
    decay = joined_decay(before[QUARTER:])
    for i in range(4):
        rows = slice(i * HD, (i + 1) * HD)
        state = before[rows] + decay[i : i + 1] * farther[rows]
        for n in range(4):
            states[n, rows, :] = state
            if n < 3:
                state = decays_ref[n, i : i + 1, :] * state + chips_ref[n, rows, :]
    a_ref[...] = states[lax.bitwise_xor(spot, 1 + 2 * core)].astype(BF16)
    b_ref[...] = states[lax.bitwise_xor(spot, 2), half_rows(core), :].astype(BF16)
    own_ref[...] = states[spot]


def inner_kernel(
    docv_ref, featc_ref, projc_ref, cum_ref, step_ref, gate_hbm, skip_hbm, gain_hbm,
    a_ref, g_ref, gain_ref, masked, gate_ref, skip_ref, sems,
):
    copies = [
        pltpu.make_async_copy(gate_hbm, gate_ref, sems.at[0]),
        pltpu.make_async_copy(skip_hbm, skip_ref, sems.at[1]),
        pltpu.make_async_copy(gain_hbm, gain_ref, sems.at[2]),
    ]
    for copy in copies:
        copy.start()
    first, start = docv_ref[0:1], docv_ref[1:2]
    scores = lax.dot_general(
        projc_ref[:, HD:], projc_ref[:, :HD], (((1,), (1,)), ((), ())),
        preferred_element_type=F32,
    )
    t = lax.broadcasted_iota(jnp.int32, (ROWS, ROWS), 0)
    s = lax.broadcasted_iota(jnp.int32, (ROWS, ROWS), 1)
    wide_start = jnp.concatenate([start, start], axis=1)
    same = (s <= t) & ((s >= wide_start) | (t < wide_start))
    masked[...] = jnp.where(same, scores, 0.0)
    cum = cum_ref[...] * LOG2E
    row_side = cum - jnp.log(step_ref[...]) * LOG2E
    padded = jnp.concatenate([cum, jnp.zeros((HD - HEADS, ROWS), F32)], axis=0)
    columns = padded.T
    t_col = lax.broadcasted_iota(jnp.int32, (ROWS, HD), 0)
    reach = (first >= 1) & ((t_col < start) | (start <= 0))
    for copy in copies:
        copy.wait()
    for h in range(HEADS):
        cols = slice(h * HD, (h + 1) * HD)
        column = jnp.broadcast_to(columns[:, h : h + 1], (ROWS, HD))
        lift = jnp.where(reach, jnp.exp2(column), 0.0)
        gate = silu(gate_ref[:, cols].astype(F32))
        g_ref[h] = gate * lift
        for top in (0, HD):
            width = top + HD
            tall = column[top : top + HD]
            wide = jnp.concatenate([tall] * (width // HD), axis=1)
            gap = jnp.minimum(wide - row_side[h : h + 1, :width], 60.0)
            weights = (masked[top : top + HD, :width] * jnp.exp2(gap)).astype(BF16)
            inner = jnp.dot(weights, featc_ref[:width, cols], preferred_element_type=F32)
            feat = featc_ref[top : top + HD, cols].astype(F32)
            a_ref[h, top : top + HD, :] = (inner + skip_ref[h] * feat) * gate[top : top + HD]


def lifted_heads(groups, second, decays, recv_ref, c, a_ref, g_ref, total, keep):
    for ref, base, count in groups:
        for i in range(count):
            h = base + i
            rows = pl.ds(pl.multiple_of(h * HD, HD), HD)
            state = ref[i * HD : (i + 1) * HD, :].astype(F32)
            middle = decays[pl.ds(h, 1), :] * state + recv_ref[rows, :].astype(F32)
            state = jnp.where(second, middle, state)
            high = state.astype(BF16)
            low = (state - high.astype(F32)).astype(BF16)
            lifted = jnp.dot(c, high, preferred_element_type=F32) + jnp.dot(
                c, low, preferred_element_type=F32
            )
            gated = a_ref[h] + lifted * g_ref[h]
            keep(h, gated)
            total = total + gated * gated
    return total


def gated_kernel(
    projc_ref, recv_ref, own_ref, fa_ref, fb_ref, a_ref, g_ref, gated_ref, total_ref, decays
):
    core = my_core()
    k = my_slice()
    decays[...] = joined_decay(recv_ref[COLS:, :])

    def keep(h, gated):
        gated_ref[h] = gated

    groups = (
        (own_ref, 4 * k, 4),
        (fa_ref, 4 * lax.bitwise_xor(k, 1 + 2 * core), 4),
        (fb_ref, 4 * lax.bitwise_xor(k, 2) + 2 * core, 2),
    )
    total_ref[...] = lifted_heads(
        groups, core == 1, decays, recv_ref, projc_ref[:, HD:], a_ref, g_ref,
        jnp.zeros((ROWS, HD), F32), keep,
    )


def last_gated_kernel(
    projc_ref, recv_ref, ha_ref, hb_ref, a_ref, g_ref, gated_in, total_ref,
    gated_ref, squares_ref, decays,
):
    del gated_in
    core = my_core()
    k = my_slice()
    decays[...] = joined_decay(recv_ref[COLS:, :])

    def keep(h, gated):
        gated_ref[h] = gated

    groups = (
        (ha_ref, 4 * lax.bitwise_xor(k, 3 - 2 * core), 4),
        (hb_ref, 4 * lax.bitwise_xor(k, 2) + 2 - 2 * core, 2),
    )
    total = lifted_heads(
        groups, core == 1, decays, recv_ref, projc_ref[:, HD:], a_ref, g_ref,
        total_ref[...], keep,
    )
    squares_ref[...] = jnp.broadcast_to(
        jnp.sum(total.T, axis=0, keepdims=True), (8, ROWS)
    )


def norm_kernel(gated_ref, s0, s1, s3, s2, gain_ref, out_hbm, out_ref, sems):
    total = (s0[0:1] + s1[0:1]) + (s2[0:1] + s3[0:1])
    scale = lax.rsqrt(total / (COLS * YS) + 1e-05)
    scale = jnp.broadcast_to(scale, (HD, ROWS)).T
    copies = []
    for i in range(HEADS):
        cols = slice(i * HD, (i + 1) * HD)
        out_ref[:, cols] = (gated_ref[i] * scale * gain_ref[0:1, cols]).astype(BF16)
        if i % 4 == 3:
            cols = pl.ds((i - 3) * HD, 4 * HD)
            copy = pltpu.make_async_copy(
                out_ref.at[:, cols], out_hbm.at[:, cols], sems.at[i // 4]
            )
            copy.start()
            copies.append(copy)
    for copy in copies:
        copy.wait()


VMEM = pl.BlockSpec(memory_space=pltpu.VMEM)
HBM = pl.BlockSpec(memory_space=pl.ANY)
DMA = pltpu.SemaphoreType.DMA


def shaped(*shape, dtype=BF16):
    return jax.ShapeDtypeStruct(shape, dtype)


def call(kernel, name, out, args, far=(), scratch=(), aliases=None, out_specs=None):
    single = not isinstance(out, (list, tuple))
    args = [
        pltpu.with_memory_space_constraint(x, pltpu.HBM) if i in far else x
        for i, x in enumerate(args)
    ]
    return pl.pallas_call(
        kernel,
        name=name,
        out_shape=out,
        in_specs=[HBM if i in far else VMEM for i in range(len(args))],
        out_specs=out_specs or (VMEM if single else [VMEM] * len(out)),
        scratch_shapes=list(scratch),
        input_output_aliases=aliases or {},
        compiler_params=pltpu.CompilerParams(vmem_limit_bytes=VMEM_LIMIT),
    )(*args)


def body(
    feat_in, gate_in, state_proj, step_raw, doc_offset, feat_taps, feat_bias,
    proj_taps, proj_bias, step_bias, decay_log, skip_gain, norm_gain,
):
    fbias = feat_bias.reshape(1, COLS)
    pbias = proj_bias.reshape(1, 256)
    gain = norm_gain.reshape(1, COLS)
    f32 = functools.partial(shaped, dtype=F32)

    params = [f32(TAPS, COLS), f32(1, COLS), f32(TAPS, 256), f32(1, 256)]
    edge, docv, feat, proj, *params, raw = call(
        edge_kernel, "edge",
        [
            shaped(16, PACK), shaped(8, HD, dtype=jnp.int32), shaped(ROWS, COLS),
            shaped(ROWS, 256), *params, f32(HEADS, ROWS),
        ],
        (doc_offset, feat_in, state_proj, feat_taps, fbias, proj_taps, pbias, step_raw),
        far=range(8),
        scratch=[pltpu.SMEM((ROWS,), jnp.int32), DMA((8,))],
    )
    rim = lax.ppermute(edge, "ctx", NEXT)

    featc, projc, cum, step, coef, decay = call(
        conv_kernel, "conv",
        [
            shaped(ROWS, COLS), shaped(ROWS, 256), f32(HEADS, ROWS), f32(HEADS, ROWS),
            f32(HEADS, ROWS), f32(HEADS, HD),
        ],
        (docv, feat, proj, *params, raw, step_bias, decay_log),
        far=(8, 9),
        scratch=[pltpu.SMEM((HEADS,), F32), pltpu.SMEM((HEADS,), F32), DMA((2,))],
    )
    featc, projc, keep, send = call(
        state_kernel, "state",
        [shaped(ROWS, COLS), shaped(ROWS, 256), f32(COLS, HD), shaped(COLS + 32, HD)],
        (docv, rim, feat, proj, *params, coef, decay, featc, projc),
        scratch=[pltpu.VMEM((32, COLS + 256), F32)],
        aliases={10: 0, 11: 1},
    )
    recv = lax.ppermute(send, "ctx", CORE)

    own, own_decay, ta, tb = call(
        chip_kernel, "chip",
        [f32(QUARTER, HD), f32(8, HD), shaped(QUARTER + 16, HD), shaped(2 * HD + 16, HD)],
        (keep, decay, recv),
        scratch=[pltpu.VMEM((40, HD), F32)],
    )
    rb = lax.ppermute(tb, "ctx", TWO)
    ra = lax.ppermute(ta, "ctx", APART)
    featc, projc, ta = lax.optimization_barrier((featc, projc, ta))
    a, g, gain = call(
        inner_kernel, "inner",
        [f32(HEADS, ROWS, HD), f32(HEADS, ROWS, HD), f32(1, COLS)],
        (docv, featc, projc, cum, step, gate_in, skip_gain, gain),
        far=(5, 6, 7),
        scratch=[
            pltpu.VMEM((ROWS, ROWS), F32),
            pltpu.VMEM((ROWS, COLS), BF16),
            pltpu.SMEM((HEADS,), F32),
            DMA((3,)),
        ],
    )
    ra, rb, a = lax.optimization_barrier((ra, rb, a))
    ga = lax.ppermute(ra, "ctx", CORE)
    gb = lax.ppermute(rb, "ctx", CORE)
    total, chips, decays = call(
        group_kernel, "group",
        [shaped(QUARTER + 16, HD), f32(4, QUARTER, HD), f32(4, 8, HD)],
        (own, own_decay, ra, ga, rb, gb),
    )
    q = lax.ppermute(total, "ctx", LATER)
    other = lax.ppermute(q, "ctx", CORE)
    e_own, ea, eb = call(
        enter_kernel, "enter",
        [f32(QUARTER, HD), shaped(QUARTER, HD), shaped(2 * HD, HD)],
        (chips, decays, q, other),
        scratch=[pltpu.VMEM((4, QUARTER, HD), F32)],
    )
    fb = lax.ppermute(eb, "ctx", TWO)
    fa = lax.ppermute(ea, "ctx", APART)
    ha = lax.ppermute(fa, "ctx", CORE)
    hb = lax.ppermute(fb, "ctx", CORE)
    gated, squares = call(
        gated_kernel, "gated", [f32(HEADS, ROWS, HD), f32(ROWS, HD)],
        (projc, recv, e_own, fa, fb, a, g), scratch=[pltpu.VMEM((HEADS, HD), F32)],
    )
    gated, squares = call(
        last_gated_kernel, "last_gated", [f32(HEADS, ROWS, HD), f32(8, ROWS)],
        (projc, recv, ha, hb, a, g, gated, squares),
        scratch=[pltpu.VMEM((HEADS, HD), F32)],
        aliases={6: 0},
    )
    s2 = lax.ppermute(squares, "head", HEAD_XOR[2])
    s3 = lax.ppermute(squares, "head", HEAD_XOR[3])
    s1 = lax.ppermute(squares, "head", HEAD_XOR[1])
    return call(
        norm_kernel, "norm", shaped(ROWS, COLS), (gated, squares, s1, s3, s2, gain),
        scratch=[pltpu.VMEM((ROWS, COLS), BF16), DMA((HEADS // 4,))],
        out_specs=HBM,
    )


def solution(mesh):
    return jax.shard_map(
        body,
        mesh=mesh,
        in_specs=(
            P("ctx", "head"),
            P("ctx", "head"),
            P("ctx", None),
            P("head", "ctx"),
            P("ctx"),
            P(None, "head"),
            P("head"),
            P(),
            P(),
            P("head"),
            P("head"),
            P("head"),
            P("head"),
        ),
        out_specs=P("ctx", "head"),
        check_vma=False,
    )
```

```python
import functools

import jax
import jax.numpy as jnp
from jax import lax
from jax.experimental import pallas as pl
from jax.experimental.pallas import tpu as pltpu
from jax.sharding import PartitionSpec as P

F32 = jnp.float32
BF16 = jnp.bfloat16
ROWS = 256
HEADS = 16
HALF = 8
HD = 128
COLS = HEADS * HD
TAPS = 4
XS, ZS, CS, YS = 4, 8, 2, 4
LOG2E = 1.4426950408889634
VMEM_LIMIT = 40 * 1024 * 1024


def spots():
    return [(x, z, c) for x in range(XS) for z in range(ZS) for c in range(CS)]


def place(x, z, c):
    return (x * ZS + z) * CS + c


def route(to):
    pairs = []
    for x, z, c in spots():
        target = to(x, z, c)
        if target is not None:
            pairs.append((place(x, z, c), place(*target)))
    return pairs


NEXT = [(i, i + 1) for i in range(XS * ZS * CS - 1)]
CORE = route(lambda x, z, c: (x, z, 1 - c))


APART = route(lambda x, z, c: (x, z ^ (1 + 2 * c), c))
TWO = route(lambda x, z, c: (x, z ^ 2, c))


def to_later_group(x, z, c):
    if c == 0 and z < 4:
        return (x, z ^ 6, c)
    if x + 1 == XS:
        return None
    return (x + 1, z ^ 6 if c == 0 else z, c)


LATER = route(to_later_group)
HEAD_XOR = {m: [(i, i ^ m) for i in range(YS)] for m in (1, 2, 3)}


def my_core():
    return lax.rem(lax.axis_index("ctx"), 2)


def my_spot():
    return lax.rem(lax.div(lax.axis_index("ctx"), 2), 4)


def my_slice():
    z = lax.rem(lax.div(lax.axis_index("ctx"), 2), ZS)
    spot = lax.rem(z, 4)
    return jnp.where(z >= 4, lax.bitwise_xor(spot, 2), spot)


def silu(v):
    half = 0.5 * v
    return half + half * jnp.tanh(half)


SOON = 10


def order_of(core):
    k = my_slice()
    apart = lax.bitwise_xor(k, 1 + 2 * core)
    two = 4 * lax.bitwise_xor(k, 2)
    later = lax.bitwise_xor(k, 3 - 2 * core)
    return (
        [4 * k + i for i in range(4)]
        + [4 * apart + i for i in range(4)]
        + [two + 2 * core + i for i in range(2)]
        + [4 * later + i for i in range(4)]
        + [two + 2 - 2 * core + i for i in range(2)]
    )


def conv_rows(xs, taps_ref, bias_ref, cols, scratch_cols, base, rows, masks):
    acc = jnp.broadcast_to(bias_ref[0:1, cols], (rows, HD))
    for k in range(TAPS):
        lag = TAPS - 1 - k
        window = xs[base - lag : base - lag + rows, scratch_cols]
        if lag:
            window = jnp.where(masks[lag], window, 0.0)
        acc = acc + taps_ref[k : k + 1, cols] * window
    return silu(acc).astype(BF16)


PACK = 640
PACKS = [(j, min(PACK, COLS + 256 - j)) for j in range(0, COLS + 256, PACK)]


def edge_kernel(
    doc_hbm, feat_hbm, proj_hbm, ftaps_hbm, fbias_hbm, ptaps_hbm, pbias_hbm, raw_hbm,
    sbias_hbm, dlog_hbm,
    out_ref, docv_ref, feat_ref, proj_ref, ftaps_ref, fbias_ref, ptaps_ref, pbias_ref, raw_ref,
    bias_ref, speed_ref, doc_ref, sbias_ref, dlog_ref, sems,
):
    tail = pl.ds(ROWS - 16, 16)
    bulk = pl.ds(0, ROWS - 16)
    copies = [
        pltpu.make_async_copy(source, target, sems.at[n])
        for n, (source, target) in enumerate((
            (feat_hbm.at[tail, :], feat_ref.at[tail, :]), (proj_hbm, proj_ref),
            (feat_hbm.at[bulk, :], feat_ref.at[bulk, :]), (doc_hbm, doc_ref),
            (ftaps_hbm, ftaps_ref), (fbias_hbm, fbias_ref), (ptaps_hbm, ptaps_ref),
            (pbias_hbm, pbias_ref), (raw_hbm, raw_ref), (sbias_hbm, sbias_ref),
            (dlog_hbm, dlog_ref),
        ))
    ]
    for copy in copies:
        copy.start()
    for copy in copies[:2]:
        copy.wait()
    last = jnp.concatenate(
        [feat_ref[ROWS - 16 :, :].astype(F32), proj_ref[ROWS - 16 :, :].astype(F32)], axis=1
    )
    last = last[16 - (TAPS - 1) :]
    rows = []
    for j, width in PACKS:
        piece = last[:, j : j + width]
        if width < PACK:
            piece = jnp.concatenate([piece, jnp.zeros((TAPS - 1, PACK - width), F32)], axis=1)
        rows.append(piece)
    rows.append(jnp.zeros((16 - (TAPS - 1) * len(PACKS), PACK), F32))
    out_ref[...] = jnp.concatenate(rows, axis=0).astype(BF16)
    for copy in copies[2:]:
        copy.wait()
    row = lax.broadcasted_iota(jnp.int32, (8, HD), 0)
    docv_ref[...] = jnp.where(row == 0, doc_ref[0], (ROWS - 1) - doc_ref[ROWS - 1])
    line = lax.broadcasted_iota(jnp.int32, (HEADS, HD), 0)
    bias = jnp.zeros((HEADS, HD), F32)
    speed = jnp.zeros((HEADS, HD), F32)
    for h in range(HEADS):
        bias = jnp.where(line == h, sbias_ref[h], bias)
        speed = jnp.where(line == h, dlog_ref[h], speed)
    bias_ref[...] = bias
    speed_ref[...] = speed


def split_decay(value):
    high = jnp.floor(value * 256.0) * (1.0 / 256.0)
    return jnp.concatenate([high, value - high], axis=0).astype(BF16)


def joined_decay(tile):
    wide = tile.astype(F32)
    half = tile.shape[0] // 2
    return wide[:half] + wide[half:]


def conv_kernel(
    docv_ref, feat_ref, proj_ref, ftaps_ref, fbias_ref, ptaps_ref, pbias_ref, raw_ref,
    sbias_ref, speed_ref,
    featc_ref, projc_ref, cum_ref, step_ref, coef_ref, decay_ref,
):
    first, start = docv_ref[0:1], docv_ref[1:2]
    first = jnp.concatenate([first, first], axis=1)
    start = jnp.concatenate([start, start], axis=1)
    t = lax.broadcasted_iota(jnp.int32, (ROWS, ROWS), 0)
    s = lax.broadcasted_iota(jnp.int32, (ROWS, ROWS), 1)
    offs = jnp.where((start > 0) & (t >= start), t - start, first + t)
    shifts = [
        jnp.where((t - s == lag) & (offs >= lag), 1.0, 0.0).astype(BF16) for lag in (1, 2, 3)
    ]

    def conv(x_ref, taps_ref, bias_ref, out_ref):
        for j in range(0, out_ref.shape[1], 256):
            cols = slice(j, j + 256)
            x = x_ref[:, cols]
            acc = jnp.broadcast_to(bias_ref[0:1, cols], (ROWS, 256))
            for k in range(TAPS):
                lag = TAPS - 1 - k
                if lag:
                    moved = jnp.dot(shifts[lag - 1], x, preferred_element_type=F32)
                else:
                    moved = x.astype(F32)
                acc = acc + taps_ref[k : k + 1, cols] * moved
            out_ref[:, cols] = silu(acc).astype(BF16)

    first, start = first[:, 0:1], start[:, 0:1]
    lane = lax.broadcasted_iota(jnp.int32, (HEADS, ROWS), 1)
    bias = sbias_ref[...]
    speed = jnp.exp(speed_ref[...])
    v = raw_ref[...] + jnp.concatenate([bias, bias], axis=1)
    step = jnp.maximum(v, 0.0) + jnp.log1p(jnp.exp(-jnp.abs(v)))
    cum = -step * jnp.concatenate([speed, speed], axis=1)
    shift = 1
    while shift < ROWS:
        cum = cum + jnp.where(lane >= shift, pltpu.roll(cum, shift, 1), 0.0)
        shift *= 2
    conv(proj_ref, ptaps_ref, pbias_ref, projc_ref)
    conv(feat_ref, ftaps_ref, fbias_ref, featc_ref)
    last = cum[:, ROWS - 1 : ROWS]
    cum_ref[...] = cum
    step_ref[...] = step
    tail = (start <= 0) | (lane >= start)
    coef_ref[...] = jnp.where(tail, jnp.exp(last - cum) * step, 0.0)
    kept = (docv_ref[1:2] < 0) & (docv_ref[0:1] >= 1)
    decay_ref[...] = jnp.where(kept, jnp.broadcast_to(jnp.exp(last), (HEADS, HD)), 0.0)


def state_kernel(
    docv_ref, rim_ref, feat_ref, proj_ref, ftaps_ref, fbias_ref, ptaps_ref, pbias_ref,
    coef_ref, decay_ref, featc_in, projc_in,
    featc_ref, projc_ref, keep_ref, send_ref, rest_ref, xs,
):
    del featc_in, projc_in
    rim = rim_ref[...].astype(F32)
    for n, (j, width) in enumerate(PACKS):
        xs[16 - (TAPS - 1) : 16, j : j + width] = rim[
            n * (TAPS - 1) : (n + 1) * (TAPS - 1), :width
        ]
    xs[16:32, :COLS] = feat_ref[0:16, :].astype(F32)
    xs[16:32, COLS:] = proj_ref[0:16, :].astype(F32)
    first, start = docv_ref[0:1], docv_ref[1:2]
    t = lax.broadcasted_iota(jnp.int32, (16, HD), 0)
    offs = jnp.where((start > 0) & (t >= start), t - start, first + t)
    masks = {lag: offs >= lag for lag in (1, 2, 3)}
    for j in range(2):
        cols = slice(j * HD, (j + 1) * HD)
        there = slice(COLS + j * HD, COLS + (j + 1) * HD)
        projc_ref[0:16, cols] = conv_rows(xs, ptaps_ref, pbias_ref, cols, there, 16, 16, masks)
    for j in range(HEADS):
        cols = slice(j * HD, (j + 1) * HD)
        featc_ref[0:16, cols] = conv_rows(xs, ftaps_ref, fbias_ref, cols, cols, 16, 16, masks)
    turned = projc_ref[:, :HD].astype(F32).T
    for n, h in enumerate(order_of(1 - my_core())):
        rows = pl.ds(pl.multiple_of(h * HD, HD), HD)
        scaled = (turned * coef_ref[pl.ds(h, 1), :]).astype(BF16)
        added = jnp.dot(scaled, featc_ref[:, rows], preferred_element_type=F32)
        keep_ref[rows, :] = added
        if n < SOON:
            send_ref[n * HD : (n + 1) * HD, :] = added.astype(BF16)
        else:
            rest_ref[(n - SOON) * HD : (n - SOON + 1) * HD, :] = added.astype(BF16)
    send_ref[SOON * HD :, :] = split_decay(decay_ref[...])


def chip_kernel(keep_ref, decay_ref, recv_ref, own_ref, own_decay_ref, a_ref, b_ref, decays):
    core = my_core()
    second = core == 1
    k = my_slice()
    theirs = joined_decay(recv_ref[SOON * HD :, :])
    mine = decay_ref[...]
    decays[0:16, :] = jnp.where(second, mine, theirs)
    decays[16:32, :] = mine * theirs
    decays[32:40, :] = jnp.zeros((8, HD), F32)

    order = order_of(core)

    def combined(n):
        h = order[n]
        a = keep_ref[pl.ds(pl.multiple_of(h * HD, HD), HD), :]
        b = recv_ref[n * HD : (n + 1) * HD, :].astype(F32)
        return decays[pl.ds(h, 1), :] * jnp.where(second, b, a) + jnp.where(second, a, b)

    for i in range(4):
        a_ref[i * HD : (i + 1) * HD, :] = combined(4 + i).astype(BF16)
    a_ref[4 * HD :, :] = split_decay(decays[pl.ds(16 + order[4], 8), :])
    for i in range(2):
        b_ref[i * HD : (i + 1) * HD, :] = combined(8 + i).astype(BF16)
    b_ref[2 * HD :, :] = split_decay(decays[pl.ds(16 + 4 * lax.bitwise_xor(k, 2), 8), :])
    for i in range(4):
        own_ref[i * HD : (i + 1) * HD, :] = combined(i)
    own_decay_ref[...] = decays[pl.ds(16 + 4 * k, 8), :]


QUARTER = 4 * HD


def half_rows(core):
    return pl.ds(pl.multiple_of(core * 2 * HD, 2 * HD), 2 * HD)


def group_kernel(
    own_ref, own_decay_ref, ra_ref, ga_ref, rb_ref, gb_ref,
    total_ref, chips_ref, decays_ref,
):
    core = my_core()
    spot = my_spot()
    chips_ref[spot] = own_ref[...]
    decays_ref[spot] = own_decay_ref[...]
    for ref, m in ((ra_ref, 1 + 2 * core), (ga_ref, 3 - 2 * core)):
        there = lax.bitwise_xor(spot, m)
        chips_ref[there] = ref[:QUARTER, :].astype(F32)
        decays_ref[there] = joined_decay(ref[QUARTER:, :])
    there = lax.bitwise_xor(spot, 2)
    chips_ref[there, half_rows(core), :] = rb_ref[: 2 * HD, :].astype(F32)
    chips_ref[there, half_rows(1 - core), :] = gb_ref[: 2 * HD, :].astype(F32)
    decays_ref[there] = joined_decay(rb_ref[2 * HD :, :])
    for i in range(4):
        rows = slice(i * HD, (i + 1) * HD)
        total = chips_ref[0, rows, :]
        for q in range(1, 4):
            total = decays_ref[q, i : i + 1, :] * total + chips_ref[q, rows, :]
        total_ref[rows, :] = total.astype(BF16)
    total_ref[QUARTER:, :] = split_decay(
        decays_ref[0] * decays_ref[1] * decays_ref[2] * decays_ref[3]
    )


def enter_kernel(chips_ref, decays_ref, q_ref, other_ref, own_ref, a_ref, b_ref, states):
    core = my_core()
    second = core == 1
    spot = my_spot()
    q = q_ref[...].astype(F32)
    other = other_ref[...].astype(F32)
    before = jnp.where(second, other, q)
    farther = jnp.where(second, q, other)
    decay = joined_decay(before[QUARTER:])
    for i in range(4):
        rows = slice(i * HD, (i + 1) * HD)
        state = before[rows] + decay[i : i + 1] * farther[rows]
        for n in range(4):
            states[n, rows, :] = state
            if n < 3:
                state = decays_ref[n, i : i + 1, :] * state + chips_ref[n, rows, :]
    a_ref[...] = states[lax.bitwise_xor(spot, 1 + 2 * core)].astype(BF16)
    b_ref[...] = states[lax.bitwise_xor(spot, 2), half_rows(core), :].astype(BF16)
    own_ref[...] = states[spot]


def inner_kernel(
    docv_ref, featc_ref, projc_ref, cum_ref, step_ref, gate_hbm, skip_hbm, gain_hbm,
    a_ref, g_ref, gain_ref, masked, gate_ref, skip_ref, sems,
):
    copies = [
        pltpu.make_async_copy(gate_hbm, gate_ref, sems.at[0]),
        pltpu.make_async_copy(skip_hbm, skip_ref, sems.at[1]),
        pltpu.make_async_copy(gain_hbm, gain_ref, sems.at[2]),
    ]
    for copy in copies:
        copy.start()
    first, start = docv_ref[0:1], docv_ref[1:2]
    scores = lax.dot_general(
        projc_ref[:, HD:], projc_ref[:, :HD], (((1,), (1,)), ((), ())),
        preferred_element_type=F32,
    )
    t = lax.broadcasted_iota(jnp.int32, (ROWS, ROWS), 0)
    s = lax.broadcasted_iota(jnp.int32, (ROWS, ROWS), 1)
    wide_start = jnp.concatenate([start, start], axis=1)
    same = (s <= t) & ((s >= wide_start) | (t < wide_start))
    masked[...] = jnp.where(same, scores, 0.0)
    cum = cum_ref[...] * LOG2E
    row_side = cum - jnp.log(step_ref[...]) * LOG2E
    padded = jnp.concatenate([cum, jnp.zeros((HD - HEADS, ROWS), F32)], axis=0)
    columns = padded.T
    t_col = lax.broadcasted_iota(jnp.int32, (ROWS, HD), 0)
    reach = (first >= 1) & ((t_col < start) | (start <= 0))
    for copy in copies:
        copy.wait()
    for h in range(HEADS):
        cols = slice(h * HD, (h + 1) * HD)
        column = jnp.broadcast_to(columns[:, h : h + 1], (ROWS, HD))
        lift = jnp.where(reach, jnp.exp2(column), 0.0)
        gate = silu(gate_ref[:, cols].astype(F32))
        g_ref[h] = gate * lift
        for top in (0, HD):
            width = top + HD
            tall = column[top : top + HD]
            wide = jnp.concatenate([tall] * (width // HD), axis=1)
            gap = jnp.minimum(wide - row_side[h : h + 1, :width], 60.0)
            weights = (masked[top : top + HD, :width] * jnp.exp2(gap)).astype(BF16)
            inner = jnp.dot(weights, featc_ref[:width, cols], preferred_element_type=F32)
            feat = featc_ref[top : top + HD, cols].astype(F32)
            a_ref[h, top : top + HD, :] = (inner + skip_ref[h] * feat) * gate[top : top + HD]


def lifted_heads(refs, heads, early_ref, decays, c, a_ref, g_ref, gated_ref, total):
    second = my_core() == 1
    states = [
        ref[i * HD : (i + 1) * HD, :] for ref in refs for i in range(ref.shape[0] // HD)
    ]
    for n, (h, state) in enumerate(zip(heads, states, strict=True)):
        state = state.astype(F32)
        early = early_ref[n * HD : (n + 1) * HD, :].astype(F32)
        state = jnp.where(second, decays[pl.ds(h, 1), :] * state + early, state)
        high = state.astype(BF16)
        low = (state - high.astype(F32)).astype(BF16)
        lifted = jnp.dot(c, high, preferred_element_type=F32) + jnp.dot(
            c, low, preferred_element_type=F32
        )
        gated = a_ref[h] + lifted * g_ref[h]
        gated_ref[h] = gated
        total = total + gated * gated
    return total


def gated_kernel(
    projc_ref, recv_ref, own_ref, fa_ref, fb_ref, a_ref, g_ref,
    gated_ref, total_ref, decays_ref,
):
    decays_ref[...] = joined_decay(recv_ref[SOON * HD :, :])
    total_ref[...] = lifted_heads(
        (own_ref, fa_ref, fb_ref), order_of(my_core())[:SOON], recv_ref, decays_ref,
        projc_ref[:, HD:], a_ref, g_ref, gated_ref, jnp.zeros((ROWS, HD), F32),
    )


def last_gated_kernel(
    projc_ref, rest_ref, decays_ref, ha_ref, hb_ref, a_ref, g_ref, gated_in, total_ref,
    gated_ref, squares_ref,
):
    del gated_in
    total = lifted_heads(
        (ha_ref, hb_ref), order_of(my_core())[SOON:], rest_ref, decays_ref,
        projc_ref[:, HD:], a_ref, g_ref, gated_ref, total_ref[...],
    )
    squares_ref[...] = jnp.broadcast_to(
        jnp.sum(total.T, axis=0, keepdims=True), (8, ROWS)
    )


def norm_kernel(gated_ref, s0, s1, s3, s2, gain_ref, out_hbm, out_ref, sems):
    total = (s0[0:1] + s1[0:1]) + (s2[0:1] + s3[0:1])
    scale = lax.rsqrt(total / (COLS * YS) + 1e-05)
    scale = jnp.broadcast_to(scale, (HD, ROWS)).T
    copies = []
    for i in range(HEADS):
        cols = slice(i * HD, (i + 1) * HD)
        out_ref[:, cols] = (gated_ref[i] * scale * gain_ref[0:1, cols]).astype(BF16)
        if i % 4 == 3:
            cols = pl.ds((i - 3) * HD, 4 * HD)
            copy = pltpu.make_async_copy(
                out_ref.at[:, cols], out_hbm.at[:, cols], sems.at[i // 4]
            )
            copy.start()
            copies.append(copy)
    for copy in copies:
        copy.wait()


VMEM = pl.BlockSpec(memory_space=pltpu.VMEM)
HBM = pl.BlockSpec(memory_space=pl.ANY)
DMA = pltpu.SemaphoreType.DMA


def shaped(*shape, dtype=BF16):
    return jax.ShapeDtypeStruct(shape, dtype)


def call(kernel, name, out, args, far=(), scratch=(), aliases=None, out_specs=None):
    single = not isinstance(out, (list, tuple))
    args = [
        pltpu.with_memory_space_constraint(x, pltpu.HBM) if i in far else x
        for i, x in enumerate(args)
    ]
    return pl.pallas_call(
        kernel,
        name=name,
        out_shape=out,
        in_specs=[HBM if i in far else VMEM for i in range(len(args))],
        out_specs=out_specs or (VMEM if single else [VMEM] * len(out)),
        scratch_shapes=list(scratch),
        input_output_aliases=aliases or {},
        compiler_params=pltpu.CompilerParams(vmem_limit_bytes=VMEM_LIMIT),
    )(*args)


def body(
    feat_in, gate_in, state_proj, step_raw, doc_offset, feat_taps, feat_bias,
    proj_taps, proj_bias, step_bias, decay_log, skip_gain, norm_gain,
):
    fbias = feat_bias.reshape(1, COLS)
    pbias = proj_bias.reshape(1, 256)
    gain = norm_gain.reshape(1, COLS)
    f32 = functools.partial(shaped, dtype=F32)

    params = [f32(TAPS, COLS), f32(1, COLS), f32(TAPS, 256), f32(1, 256)]
    edge, docv, feat, proj, *params, raw, bias, speed = call(
        edge_kernel, "edge",
        [
            shaped(16, PACK), shaped(8, HD, dtype=jnp.int32), shaped(ROWS, COLS),
            shaped(ROWS, 256), *params, f32(HEADS, ROWS), f32(HEADS, HD), f32(HEADS, HD),
        ],
        (
            doc_offset, feat_in, state_proj, feat_taps, fbias, proj_taps, pbias, step_raw,
            step_bias, decay_log,
        ),
        far=range(10),
        scratch=[
            pltpu.SMEM((ROWS,), jnp.int32), pltpu.SMEM((HEADS,), F32),
            pltpu.SMEM((HEADS,), F32), DMA((11,)),
        ],
    )
    rim = lax.ppermute(edge, "ctx", NEXT)

    featc, projc, cum, step, coef, decay = call(
        conv_kernel, "conv",
        [
            shaped(ROWS, COLS), shaped(ROWS, 256), f32(HEADS, ROWS), f32(HEADS, ROWS),
            f32(HEADS, ROWS), f32(HEADS, HD),
        ],
        (docv, feat, proj, *params, raw, bias, speed),
    )
    featc, projc, keep, send, rest = call(
        state_kernel, "state",
        [
            shaped(ROWS, COLS), shaped(ROWS, 256), f32(COLS, HD), shaped(SOON * HD + 32, HD),
            shaped((HEADS - SOON) * HD, HD),
        ],
        (docv, rim, feat, proj, *params, coef, decay, featc, projc),
        scratch=[pltpu.VMEM((32, COLS + 256), F32)],
        aliases={10: 0, 11: 1},
    )
    recv = lax.ppermute(send, "ctx", CORE)

    own, own_decay, ta, tb = call(
        chip_kernel, "chip",
        [f32(QUARTER, HD), f32(8, HD), shaped(QUARTER + 16, HD), shaped(2 * HD + 16, HD)],
        (keep, decay, recv),
        scratch=[pltpu.VMEM((40, HD), F32)],
    )
    rb = lax.ppermute(tb, "ctx", TWO)
    ra = lax.ppermute(ta, "ctx", APART)
    featc, projc, ta = lax.optimization_barrier((featc, projc, ta))
    a, g, gain = call(
        inner_kernel, "inner",
        [f32(HEADS, ROWS, HD), f32(HEADS, ROWS, HD), f32(1, COLS)],
        (docv, featc, projc, cum, step, gate_in, skip_gain, gain),
        far=(5, 6, 7),
        scratch=[
            pltpu.VMEM((ROWS, ROWS), F32),
            pltpu.VMEM((ROWS, COLS), BF16),
            pltpu.SMEM((HEADS,), F32),
            DMA((3,)),
        ],
    )
    ra, rb, a = lax.optimization_barrier((ra, rb, a))
    ga = lax.ppermute(ra, "ctx", CORE)
    gb = lax.ppermute(rb, "ctx", CORE)
    total, chips, decays = call(
        group_kernel, "group",
        [shaped(QUARTER + 16, HD), f32(4, QUARTER, HD), f32(4, 8, HD)],
        (own, own_decay, ra, ga, rb, gb),
    )
    q = lax.ppermute(total, "ctx", LATER)
    rest, chips = lax.optimization_barrier((rest, chips))
    rest = lax.ppermute(rest, "ctx", CORE)
    other = lax.ppermute(q, "ctx", CORE)
    other, rest = lax.optimization_barrier((other, rest))
    e_own, ea, eb = call(
        enter_kernel, "enter",
        [f32(QUARTER, HD), shaped(QUARTER, HD), shaped(2 * HD, HD)],
        (chips, decays, q, other),
        scratch=[pltpu.VMEM((4, QUARTER, HD), F32)],
    )
    fb = lax.ppermute(eb, "ctx", TWO)
    fa = lax.ppermute(ea, "ctx", APART)
    ha = lax.ppermute(fa, "ctx", CORE)
    hb = lax.ppermute(fb, "ctx", CORE)
    gated, squares, early_decay = call(
        gated_kernel, "gated", [f32(HEADS, ROWS, HD), f32(ROWS, HD), f32(HEADS, HD)],
        (projc, recv, e_own, fa, fb, a, g),
    )
    gated, squares = call(
        last_gated_kernel, "last_gated", [f32(HEADS, ROWS, HD), f32(8, ROWS)],
        (projc, rest, early_decay, ha, hb, a, g, gated, squares),
        aliases={7: 0},
    )
    s2 = lax.ppermute(squares, "head", HEAD_XOR[2])
    s3 = lax.ppermute(squares, "head", HEAD_XOR[3])
    s1 = lax.ppermute(squares, "head", HEAD_XOR[1])
    return call(
        norm_kernel, "norm", shaped(ROWS, COLS), (gated, squares, s1, s3, s2, gain),
        scratch=[pltpu.VMEM((ROWS, COLS), BF16), DMA((HEADS // 4,))],
        out_specs=HBM,
    )


def solution(mesh):
    return jax.shard_map(
        body,
        mesh=mesh,
        in_specs=(
            P("ctx", "head"),
            P("ctx", "head"),
            P("ctx", None),
            P("head", "ctx"),
            P("ctx"),
            P(None, "head"),
            P("head"),
            P(),
            P(),
            P("head"),
            P("head"),
            P("head"),
            P("head"),
        ),
        out_specs=P("ctx", "head"),
        check_vma=False,
    )
```

```python
import functools

import jax
import jax.numpy as jnp
from jax import lax
from jax.experimental import pallas as pl
from jax.experimental.pallas import tpu as pltpu
from jax.sharding import PartitionSpec as P

F32 = jnp.float32
BF16 = jnp.bfloat16
ROWS = 256
HEADS = 16
HALF = 8
HD = 128
COLS = HEADS * HD
TAPS = 4
XS, ZS, CS, YS = 4, 8, 2, 4
LOG2E = 1.4426950408889634
VMEM_LIMIT = 40 * 1024 * 1024


def spots():
    return [(x, z, c) for x in range(XS) for z in range(ZS) for c in range(CS)]


def place(x, z, c):
    return (x * ZS + z) * CS + c


def route(to):
    pairs = []
    for x, z, c in spots():
        target = to(x, z, c)
        if target is not None:
            pairs.append((place(x, z, c), place(*target)))
    return pairs


NEXT = [(i, i + 1) for i in range(XS * ZS * CS - 1)]
CORE = route(lambda x, z, c: (x, z, 1 - c))


APART = route(lambda x, z, c: (x, z ^ (1 + 2 * c), c))
TWO = route(lambda x, z, c: (x, z ^ 2, c))


def to_later_group(x, z, c):
    if c == 0 and z < 4:
        return (x, z ^ 6, c)
    if x + 1 == XS:
        return None
    return (x + 1, z ^ 6 if c == 0 else z, c)


LATER = route(to_later_group)
HEAD_XOR = {m: [(i, i ^ m) for i in range(YS)] for m in (1, 2, 3)}


def my_core():
    return lax.rem(lax.axis_index("ctx"), 2)


def my_spot():
    return lax.rem(lax.div(lax.axis_index("ctx"), 2), 4)


def my_slice():
    z = lax.rem(lax.div(lax.axis_index("ctx"), 2), ZS)
    spot = lax.rem(z, 4)
    return jnp.where(z >= 4, lax.bitwise_xor(spot, 2), spot)


def silu(v):
    half = 0.5 * v
    return half + half * jnp.tanh(half)


SOON = 10


def order_of(core):
    k = my_slice()
    apart = lax.bitwise_xor(k, 1 + 2 * core)
    two = 4 * lax.bitwise_xor(k, 2)
    later = lax.bitwise_xor(k, 3 - 2 * core)
    return (
        [4 * k + i for i in range(4)]
        + [4 * apart + i for i in range(4)]
        + [two + 2 * core + i for i in range(2)]
        + [4 * later + i for i in range(4)]
        + [two + 2 - 2 * core + i for i in range(2)]
    )


def conv_rows(xs, taps_ref, bias_ref, cols, scratch_cols, base, rows, masks):
    acc = jnp.broadcast_to(bias_ref[0:1, cols], (rows, HD))
    for k in range(TAPS):
        lag = TAPS - 1 - k
        window = xs[base - lag : base - lag + rows, scratch_cols]
        if lag:
            window = jnp.where(masks[lag], window, 0.0)
        acc = acc + taps_ref[k : k + 1, cols] * window
    return silu(acc).astype(BF16)


PACK = 640
PACKS = [(j, min(PACK, COLS + 256 - j)) for j in range(0, COLS + 256, PACK)]


def edge_kernel(
    doc_hbm, feat_hbm, proj_hbm, ftaps_hbm, fbias_hbm, ptaps_hbm, pbias_hbm, raw_hbm,
    sbias_hbm, dlog_hbm,
    out_ref, docv_ref, feat_ref, proj_ref, ftaps_ref, fbias_ref, ptaps_ref, pbias_ref, raw_ref,
    bias_ref, speed_ref, doc_ref, sbias_ref, dlog_ref, sems,
):
    tail = pl.ds(ROWS - 16, 16)
    bulk = pl.ds(0, ROWS - 16)
    copies = [
        pltpu.make_async_copy(source, target, sems.at[n])
        for n, (source, target) in enumerate((
            (feat_hbm.at[tail, :], feat_ref.at[tail, :]), (proj_hbm, proj_ref),
            (feat_hbm.at[bulk, :], feat_ref.at[bulk, :]), (doc_hbm, doc_ref),
            (ftaps_hbm, ftaps_ref), (fbias_hbm, fbias_ref), (ptaps_hbm, ptaps_ref),
            (pbias_hbm, pbias_ref), (raw_hbm, raw_ref), (sbias_hbm, sbias_ref),
            (dlog_hbm, dlog_ref),
        ))
    ]
    for copy in copies:
        copy.start()
    for copy in copies[:2]:
        copy.wait()
    last = jnp.concatenate(
        [feat_ref[ROWS - 16 :, :].astype(F32), proj_ref[ROWS - 16 :, :].astype(F32)], axis=1
    )
    last = last[16 - (TAPS - 1) :]
    rows = []
    for j, width in PACKS:
        piece = last[:, j : j + width]
        if width < PACK:
            piece = jnp.concatenate([piece, jnp.zeros((TAPS - 1, PACK - width), F32)], axis=1)
        rows.append(piece)
    rows.append(jnp.zeros((16 - (TAPS - 1) * len(PACKS), PACK), F32))
    out_ref[...] = jnp.concatenate(rows, axis=0).astype(BF16)
    for copy in copies[2:]:
        copy.wait()
    row = lax.broadcasted_iota(jnp.int32, (8, HD), 0)
    docv_ref[...] = jnp.where(row == 0, doc_ref[0], (ROWS - 1) - doc_ref[ROWS - 1])
    line = lax.broadcasted_iota(jnp.int32, (HEADS, HD), 0)
    bias = jnp.zeros((HEADS, HD), F32)
    speed = jnp.zeros((HEADS, HD), F32)
    for h in range(HEADS):
        bias = jnp.where(line == h, sbias_ref[h], bias)
        speed = jnp.where(line == h, dlog_ref[h], speed)
    bias_ref[...] = bias
    speed_ref[...] = speed


def split_decay(value):
    high = jnp.floor(value * 256.0) * (1.0 / 256.0)
    return jnp.concatenate([high, value - high], axis=0).astype(BF16)


def joined_decay(tile):
    wide = tile.astype(F32)
    half = tile.shape[0] // 2
    return wide[:half] + wide[half:]


def conv_kernel(
    docv_ref, feat_ref, proj_ref, ftaps_ref, fbias_ref, ptaps_ref, pbias_ref, raw_ref,
    sbias_ref, speed_ref,
    featc_ref, projc_ref, cum_ref, step_ref, coef_ref, decay_ref,
):
    first, start = docv_ref[0:1], docv_ref[1:2]
    first = jnp.concatenate([first, first], axis=1)
    start = jnp.concatenate([start, start], axis=1)
    t = lax.broadcasted_iota(jnp.int32, (ROWS, ROWS), 0)
    s = lax.broadcasted_iota(jnp.int32, (ROWS, ROWS), 1)
    offs = jnp.where((start > 0) & (t >= start), t - start, first + t)
    shifts = [
        jnp.where((t - s == lag) & (offs >= lag), 1.0, 0.0).astype(BF16) for lag in (1, 2, 3)
    ]

    def conv(x_ref, taps_ref, bias_ref, out_ref):
        for j in range(0, out_ref.shape[1], 256):
            cols = slice(j, j + 256)
            x = x_ref[:, cols]
            acc = jnp.broadcast_to(bias_ref[0:1, cols], (ROWS, 256))
            for k in range(TAPS):
                lag = TAPS - 1 - k
                if lag:
                    moved = jnp.dot(shifts[lag - 1], x, preferred_element_type=F32)
                else:
                    moved = x.astype(F32)
                acc = acc + taps_ref[k : k + 1, cols] * moved
            out_ref[:, cols] = silu(acc).astype(BF16)

    first, start = first[:, 0:1], start[:, 0:1]
    lane = lax.broadcasted_iota(jnp.int32, (HEADS, ROWS), 1)
    bias = sbias_ref[...]
    speed = jnp.exp(speed_ref[...])
    v = raw_ref[...] + jnp.concatenate([bias, bias], axis=1)
    step = jnp.maximum(v, 0.0) + jnp.log1p(jnp.exp(-jnp.abs(v)))
    cum = -step * jnp.concatenate([speed, speed], axis=1)
    shift = 1
    while shift < ROWS:
        cum = cum + jnp.where(lane >= shift, pltpu.roll(cum, shift, 1), 0.0)
        shift *= 2
    conv(proj_ref, ptaps_ref, pbias_ref, projc_ref)
    conv(feat_ref, ftaps_ref, fbias_ref, featc_ref)
    last = cum[:, ROWS - 1 : ROWS]
    cum_ref[...] = cum
    step_ref[...] = step
    tail = (start <= 0) | (lane >= start)
    coef_ref[...] = jnp.where(tail, jnp.exp(last - cum) * step, 0.0)
    kept = (docv_ref[1:2] < 0) & (docv_ref[0:1] >= 1)
    decay_ref[...] = jnp.where(kept, jnp.broadcast_to(jnp.exp(last), (HEADS, HD)), 0.0)


def state_kernel(
    docv_ref, rim_ref, feat_ref, proj_ref, ftaps_ref, fbias_ref, ptaps_ref, pbias_ref,
    coef_ref, decay_ref, featc_in, projc_in,
    featc_ref, projc_ref, keep_ref, send_ref, rest_ref, xs,
):
    del featc_in, projc_in
    rim = rim_ref[...].astype(F32)
    for n, (j, width) in enumerate(PACKS):
        xs[16 - (TAPS - 1) : 16, j : j + width] = rim[
            n * (TAPS - 1) : (n + 1) * (TAPS - 1), :width
        ]
    xs[16:32, :COLS] = feat_ref[0:16, :].astype(F32)
    xs[16:32, COLS:] = proj_ref[0:16, :].astype(F32)
    first, start = docv_ref[0:1], docv_ref[1:2]
    t = lax.broadcasted_iota(jnp.int32, (16, HD), 0)
    offs = jnp.where((start > 0) & (t >= start), t - start, first + t)
    masks = {lag: offs >= lag for lag in (1, 2, 3)}
    for j in range(2):
        cols = slice(j * HD, (j + 1) * HD)
        there = slice(COLS + j * HD, COLS + (j + 1) * HD)
        projc_ref[0:16, cols] = conv_rows(xs, ptaps_ref, pbias_ref, cols, there, 16, 16, masks)
    for j in range(HEADS):
        cols = slice(j * HD, (j + 1) * HD)
        featc_ref[0:16, cols] = conv_rows(xs, ftaps_ref, fbias_ref, cols, cols, 16, 16, masks)
    turned = projc_ref[:, :HD].astype(F32).T
    for n, h in enumerate(order_of(1 - my_core())):
        rows = pl.ds(pl.multiple_of(h * HD, HD), HD)
        scaled = (turned * coef_ref[pl.ds(h, 1), :]).astype(BF16)
        added = jnp.dot(scaled, featc_ref[:, rows], preferred_element_type=F32)
        keep_ref[rows, :] = added
        if n < SOON:
            send_ref[n * HD : (n + 1) * HD, :] = added.astype(BF16)
        else:
            rest_ref[(n - SOON) * HD : (n - SOON + 1) * HD, :] = added.astype(BF16)
    send_ref[SOON * HD :, :] = split_decay(decay_ref[...])


def chip_kernel(keep_ref, decay_ref, recv_ref, own_ref, own_decay_ref, a_ref, b_ref, decays):
    core = my_core()
    second = core == 1
    k = my_slice()
    theirs = joined_decay(recv_ref[SOON * HD :, :])
    mine = decay_ref[...]
    decays[0:16, :] = jnp.where(second, mine, theirs)
    decays[16:32, :] = mine * theirs
    decays[32:40, :] = jnp.zeros((8, HD), F32)

    order = order_of(core)

    def combined(n):
        h = order[n]
        a = keep_ref[pl.ds(pl.multiple_of(h * HD, HD), HD), :]
        b = recv_ref[n * HD : (n + 1) * HD, :].astype(F32)
        return decays[pl.ds(h, 1), :] * jnp.where(second, b, a) + jnp.where(second, a, b)

    for i in range(4):
        a_ref[i * HD : (i + 1) * HD, :] = combined(4 + i).astype(BF16)
    a_ref[4 * HD :, :] = split_decay(decays[pl.ds(16 + order[4], 8), :])
    for i in range(2):
        b_ref[i * HD : (i + 1) * HD, :] = combined(8 + i).astype(BF16)
    b_ref[2 * HD :, :] = split_decay(decays[pl.ds(16 + 4 * lax.bitwise_xor(k, 2), 8), :])
    for i in range(4):
        own_ref[i * HD : (i + 1) * HD, :] = combined(i)
    own_decay_ref[...] = decays[pl.ds(16 + 4 * k, 8), :]


QUARTER = 4 * HD


def half_rows(core):
    return pl.ds(pl.multiple_of(core * 2 * HD, 2 * HD), 2 * HD)


def group_kernel(
    own_ref, own_decay_ref, ra_ref, ga_ref, rb_ref, gb_ref,
    total_ref, chips_ref, decays_ref,
):
    core = my_core()
    spot = my_spot()
    chips_ref[spot] = own_ref[...]
    decays_ref[spot] = own_decay_ref[...]
    for ref, m in ((ra_ref, 1 + 2 * core), (ga_ref, 3 - 2 * core)):
        there = lax.bitwise_xor(spot, m)
        chips_ref[there] = ref[:QUARTER, :].astype(F32)
        decays_ref[there] = joined_decay(ref[QUARTER:, :])
    there = lax.bitwise_xor(spot, 2)
    chips_ref[there, half_rows(core), :] = rb_ref[: 2 * HD, :].astype(F32)
    chips_ref[there, half_rows(1 - core), :] = gb_ref[: 2 * HD, :].astype(F32)
    decays_ref[there] = joined_decay(rb_ref[2 * HD :, :])
    for i in range(4):
        rows = slice(i * HD, (i + 1) * HD)
        total = chips_ref[0, rows, :]
        for q in range(1, 4):
            total = decays_ref[q, i : i + 1, :] * total + chips_ref[q, rows, :]
        total_ref[rows, :] = total.astype(BF16)
    total_ref[QUARTER:, :] = split_decay(
        decays_ref[0] * decays_ref[1] * decays_ref[2] * decays_ref[3]
    )


def enter_kernel(chips_ref, decays_ref, q_ref, other_ref, own_ref, a_ref, b_ref, states):
    core = my_core()
    second = core == 1
    spot = my_spot()
    q = q_ref[...].astype(F32)
    other = other_ref[...].astype(F32)
    before = jnp.where(second, other, q)
    farther = jnp.where(second, q, other)
    decay = joined_decay(before[QUARTER:])
    for i in range(4):
        rows = slice(i * HD, (i + 1) * HD)
        state = before[rows] + decay[i : i + 1] * farther[rows]
        for n in range(4):
            states[n, rows, :] = state
            if n < 3:
                state = decays_ref[n, i : i + 1, :] * state + chips_ref[n, rows, :]
    a_ref[...] = states[lax.bitwise_xor(spot, 1 + 2 * core)].astype(BF16)
    b_ref[...] = states[lax.bitwise_xor(spot, 2), half_rows(core), :].astype(BF16)
    own_ref[...] = states[spot]


def inner_kernel(
    docv_ref, featc_ref, projc_ref, cum_ref, step_ref, gate_hbm, skip_hbm, gain_hbm,
    a_ref, g_ref, gain_ref, masked, gate_ref, skip_ref, sems,
):
    copies = [
        pltpu.make_async_copy(gate_hbm, gate_ref, sems.at[0]),
        pltpu.make_async_copy(skip_hbm, skip_ref, sems.at[1]),
        pltpu.make_async_copy(gain_hbm, gain_ref, sems.at[2]),
    ]
    for copy in copies:
        copy.start()
    first, start = docv_ref[0:1], docv_ref[1:2]
    scores = lax.dot_general(
        projc_ref[:, HD:], projc_ref[:, :HD], (((1,), (1,)), ((), ())),
        preferred_element_type=F32,
    )
    t = lax.broadcasted_iota(jnp.int32, (ROWS, ROWS), 0)
    s = lax.broadcasted_iota(jnp.int32, (ROWS, ROWS), 1)
    wide_start = jnp.concatenate([start, start], axis=1)
    same = (s <= t) & ((s >= wide_start) | (t < wide_start))
    masked[...] = jnp.where(same, scores, 0.0)
    cum = cum_ref[...] * LOG2E
    row_side = cum - jnp.log(step_ref[...]) * LOG2E
    padded = jnp.concatenate([cum, jnp.zeros((HD - HEADS, ROWS), F32)], axis=0)
    columns = padded.T
    t_col = lax.broadcasted_iota(jnp.int32, (ROWS, HD), 0)
    reach = (first >= 1) & ((t_col < start) | (start <= 0))
    for copy in copies:
        copy.wait()
    for h in range(HEADS):
        cols = slice(h * HD, (h + 1) * HD)
        column = jnp.broadcast_to(columns[:, h : h + 1], (ROWS, HD))
        lift = jnp.where(reach, jnp.exp2(column), 0.0)
        gate = silu(gate_ref[:, cols].astype(F32))
        g_ref[h] = gate * lift
        for top in (0, HD):
            width = top + HD
            tall = column[top : top + HD]
            wide = jnp.concatenate([tall] * (width // HD), axis=1)
            gap = jnp.minimum(wide - row_side[h : h + 1, :width], 60.0)
            weights = (masked[top : top + HD, :width] * jnp.exp2(gap)).astype(BF16)
            inner = jnp.dot(weights, featc_ref[:width, cols], preferred_element_type=F32)
            feat = featc_ref[top : top + HD, cols].astype(F32)
            a_ref[h, top : top + HD, :] = (inner + skip_ref[h] * feat) * gate[top : top + HD]


def lifted_heads(refs, heads, early_ref, decays, c, a_ref, g_ref, gain_ref, gated_ref, total):
    second = my_core() == 1
    states = [
        ref[i * HD : (i + 1) * HD, :] for ref in refs for i in range(ref.shape[0] // HD)
    ]
    for n, (h, state) in enumerate(zip(heads, states, strict=True)):
        state = state.astype(F32)
        early = early_ref[n * HD : (n + 1) * HD, :].astype(F32)
        state = jnp.where(second, decays[pl.ds(h, 1), :] * state + early, state)
        high = state.astype(BF16)
        low = (state - high.astype(F32)).astype(BF16)
        lifted = jnp.dot(c, high, preferred_element_type=F32) + jnp.dot(
            c, low, preferred_element_type=F32
        )
        gated = a_ref[h] + lifted * g_ref[h]
        cols = pl.ds(pl.multiple_of(h * HD, HD), HD)
        gated_ref[h] = gated * gain_ref[0:1, cols]
        total = total + gated * gated
    return total


def gated_kernel(
    projc_ref, recv_ref, own_ref, fa_ref, fb_ref, a_ref, g_ref, gain_ref,
    gated_ref, total_ref, decays_ref,
):
    decays_ref[...] = joined_decay(recv_ref[SOON * HD :, :])
    total_ref[...] = lifted_heads(
        (own_ref, fa_ref, fb_ref), order_of(my_core())[:SOON], recv_ref, decays_ref,
        projc_ref[:, HD:], a_ref, g_ref, gain_ref, gated_ref, jnp.zeros((ROWS, HD), F32),
    )


def last_gated_kernel(
    projc_ref, rest_ref, decays_ref, ha_ref, hb_ref, a_ref, g_ref, gain_ref, gated_in, total_ref,
    gated_ref, squares_ref,
):
    del gated_in
    total = lifted_heads(
        (ha_ref, hb_ref), order_of(my_core())[SOON:], rest_ref, decays_ref,
        projc_ref[:, HD:], a_ref, g_ref, gain_ref, gated_ref, total_ref[...],
    )
    squares_ref[...] = jnp.broadcast_to(
        jnp.sum(total.T, axis=0, keepdims=True), (8, ROWS)
    )


def norm_kernel(gated_ref, s0, s1, s3, s2, out_hbm, out_ref, sems):
    total = (s0[0:1] + s1[0:1]) + (s2[0:1] + s3[0:1])
    scale = lax.rsqrt(total / (COLS * YS) + 1e-05)
    scale = jnp.broadcast_to(scale, (HD, ROWS)).T
    copies = []
    for i in range(HEADS):
        cols = slice(i * HD, (i + 1) * HD)
        out_ref[:, cols] = (gated_ref[i] * scale).astype(BF16)
        if i % 2 == 1:
            cols = pl.ds((i - 1) * HD, 2 * HD)
            copy = pltpu.make_async_copy(
                out_ref.at[:, cols], out_hbm.at[:, cols], sems.at[i // 2]
            )
            copy.start()
            copies.append(copy)
    for copy in copies:
        copy.wait()


VMEM = pl.BlockSpec(memory_space=pltpu.VMEM)
HBM = pl.BlockSpec(memory_space=pl.ANY)
DMA = pltpu.SemaphoreType.DMA


def shaped(*shape, dtype=BF16):
    return jax.ShapeDtypeStruct(shape, dtype)


def call(kernel, name, out, args, far=(), scratch=(), aliases=None, out_specs=None):
    single = not isinstance(out, (list, tuple))
    args = [
        pltpu.with_memory_space_constraint(x, pltpu.HBM) if i in far else x
        for i, x in enumerate(args)
    ]
    return pl.pallas_call(
        kernel,
        name=name,
        out_shape=out,
        in_specs=[HBM if i in far else VMEM for i in range(len(args))],
        out_specs=out_specs or (VMEM if single else [VMEM] * len(out)),
        scratch_shapes=list(scratch),
        input_output_aliases=aliases or {},
        compiler_params=pltpu.CompilerParams(vmem_limit_bytes=VMEM_LIMIT),
    )(*args)


def body(
    feat_in, gate_in, state_proj, step_raw, doc_offset, feat_taps, feat_bias,
    proj_taps, proj_bias, step_bias, decay_log, skip_gain, norm_gain,
):
    fbias = feat_bias.reshape(1, COLS)
    pbias = proj_bias.reshape(1, 256)
    gain = norm_gain.reshape(1, COLS)
    f32 = functools.partial(shaped, dtype=F32)

    params = [f32(TAPS, COLS), f32(1, COLS), f32(TAPS, 256), f32(1, 256)]
    edge, docv, feat, proj, *params, raw, bias, speed = call(
        edge_kernel, "edge",
        [
            shaped(16, PACK), shaped(8, HD, dtype=jnp.int32), shaped(ROWS, COLS),
            shaped(ROWS, 256), *params, f32(HEADS, ROWS), f32(HEADS, HD), f32(HEADS, HD),
        ],
        (
            doc_offset, feat_in, state_proj, feat_taps, fbias, proj_taps, pbias, step_raw,
            step_bias, decay_log,
        ),
        far=range(10),
        scratch=[
            pltpu.SMEM((ROWS,), jnp.int32), pltpu.SMEM((HEADS,), F32),
            pltpu.SMEM((HEADS,), F32), DMA((11,)),
        ],
    )
    rim = lax.ppermute(edge, "ctx", NEXT)

    featc, projc, cum, step, coef, decay = call(
        conv_kernel, "conv",
        [
            shaped(ROWS, COLS), shaped(ROWS, 256), f32(HEADS, ROWS), f32(HEADS, ROWS),
            f32(HEADS, ROWS), f32(HEADS, HD),
        ],
        (docv, feat, proj, *params, raw, bias, speed),
    )
    featc, projc, keep, send, rest = call(
        state_kernel, "state",
        [
            shaped(ROWS, COLS), shaped(ROWS, 256), f32(COLS, HD), shaped(SOON * HD + 32, HD),
            shaped((HEADS - SOON) * HD, HD),
        ],
        (docv, rim, feat, proj, *params, coef, decay, featc, projc),
        scratch=[pltpu.VMEM((32, COLS + 256), F32)],
        aliases={10: 0, 11: 1},
    )
    recv = lax.ppermute(send, "ctx", CORE)

    own, own_decay, ta, tb = call(
        chip_kernel, "chip",
        [f32(QUARTER, HD), f32(8, HD), shaped(QUARTER + 16, HD), shaped(2 * HD + 16, HD)],
        (keep, decay, recv),
        scratch=[pltpu.VMEM((40, HD), F32)],
    )
    rb = lax.ppermute(tb, "ctx", TWO)
    ra = lax.ppermute(ta, "ctx", APART)
    featc, projc, ta = lax.optimization_barrier((featc, projc, ta))
    a, g, gain = call(
        inner_kernel, "inner",
        [f32(HEADS, ROWS, HD), f32(HEADS, ROWS, HD), f32(1, COLS)],
        (docv, featc, projc, cum, step, gate_in, skip_gain, gain),
        far=(5, 6, 7),
        scratch=[
            pltpu.VMEM((ROWS, ROWS), F32),
            pltpu.VMEM((ROWS, COLS), BF16),
            pltpu.SMEM((HEADS,), F32),
            DMA((3,)),
        ],
    )
    ra, a = lax.optimization_barrier((ra, a))
    ga = lax.ppermute(ra, "ctx", CORE)
    gb = lax.ppermute(rb, "ctx", CORE)
    total, chips, decays = call(
        group_kernel, "group",
        [shaped(QUARTER + 16, HD), f32(4, QUARTER, HD), f32(4, 8, HD)],
        (own, own_decay, ra, ga, rb, gb),
    )
    q = lax.ppermute(total, "ctx", LATER)
    rest, chips = lax.optimization_barrier((rest, chips))
    rest = lax.ppermute(rest, "ctx", CORE)
    other = lax.ppermute(q, "ctx", CORE)
    other, rest = lax.optimization_barrier((other, rest))
    e_own, ea, eb = call(
        enter_kernel, "enter",
        [f32(QUARTER, HD), shaped(QUARTER, HD), shaped(2 * HD, HD)],
        (chips, decays, q, other),
        scratch=[pltpu.VMEM((4, QUARTER, HD), F32)],
    )
    fb = lax.ppermute(eb, "ctx", TWO)
    fa = lax.ppermute(ea, "ctx", APART)
    ha = lax.ppermute(fa, "ctx", CORE)
    hb = lax.ppermute(fb, "ctx", CORE)
    gated, squares, early_decay = call(
        gated_kernel, "gated", [f32(HEADS, ROWS, HD), f32(ROWS, HD), f32(HEADS, HD)],
        (projc, recv, e_own, fa, fb, a, g, gain),
    )
    gated, squares = call(
        last_gated_kernel, "last_gated", [f32(HEADS, ROWS, HD), f32(8, ROWS)],
        (projc, rest, early_decay, ha, hb, a, g, gain, gated, squares),
        aliases={8: 0},
    )
    s2 = lax.ppermute(squares, "head", HEAD_XOR[2])
    s3 = lax.ppermute(squares, "head", HEAD_XOR[3])
    s1 = lax.ppermute(squares, "head", HEAD_XOR[1])
    return call(
        norm_kernel, "norm", shaped(ROWS, COLS), (gated, squares, s1, s3, s2),
        scratch=[pltpu.VMEM((ROWS, COLS), BF16), DMA((HEADS // 2,))],
        out_specs=HBM,
    )


def solution(mesh):
    return jax.shard_map(
        body,
        mesh=mesh,
        in_specs=(
            P("ctx", "head"),
            P("ctx", "head"),
            P("ctx", None),
            P("head", "ctx"),
            P("ctx"),
            P(None, "head"),
            P("head"),
            P(),
            P(),
            P("head"),
            P("head"),
            P("head"),
            P("head"),
        ),
        out_specs=P("ctx", "head"),
        check_vma=False,
    )
```

```python
import functools

import jax
import jax.numpy as jnp
from jax import lax
from jax.experimental import pallas as pl
from jax.experimental.pallas import tpu as pltpu
from jax.sharding import PartitionSpec as P

F32 = jnp.float32
BF16 = jnp.bfloat16
ROWS = 256
HEADS = 16
HALF = 8
HD = 128
COLS = HEADS * HD
TAPS = 4
XS, ZS, CS, YS = 4, 8, 2, 4
LOG2E = 1.4426950408889634
VMEM_LIMIT = 40 * 1024 * 1024


def spots():
    return [(x, z, c) for x in range(XS) for z in range(ZS) for c in range(CS)]


def place(x, z, c):
    return (x * ZS + z) * CS + c


def route(to):
    pairs = []
    for x, z, c in spots():
        target = to(x, z, c)
        if target is not None:
            pairs.append((place(x, z, c), place(*target)))
    return pairs


NEXT = [(i, i + 1) for i in range(XS * ZS * CS - 1)]
CORE = route(lambda x, z, c: (x, z, 1 - c))


APART = route(lambda x, z, c: (x, z ^ (1 + 2 * c), c))
TWO = route(lambda x, z, c: (x, z ^ 2, c))


def to_later_group(x, z, c):
    if c == 0 and z < 4:
        return (x, z ^ 6, c)
    return ((x + 1) % XS, z ^ 6 if c == 0 else z, c)


LATER = route(to_later_group)
HEAD_XOR = {m: [(i, i ^ m) for i in range(YS)] for m in (1, 2, 3)}


def my_core():
    return lax.rem(lax.axis_index("ctx"), 2)


def my_spot():
    return lax.rem(lax.div(lax.axis_index("ctx"), 2), 4)


def my_slice():
    z = lax.rem(lax.div(lax.axis_index("ctx"), 2), ZS)
    spot = lax.rem(z, 4)
    return jnp.where(z >= 4, lax.bitwise_xor(spot, 2), spot)


def silu(v):
    half = 0.5 * v
    return half + half * jnp.tanh(half)


SOON = 10


def order_of(core):
    k = my_slice()
    apart = lax.bitwise_xor(k, 1 + 2 * core)
    two = 4 * lax.bitwise_xor(k, 2)
    later = lax.bitwise_xor(k, 3 - 2 * core)
    return (
        [4 * k + i for i in range(4)]
        + [4 * apart + i for i in range(4)]
        + [two + 2 * core + i for i in range(2)]
        + [4 * later + i for i in range(4)]
        + [two + 2 - 2 * core + i for i in range(2)]
    )


def conv_rows(xs, taps_ref, bias_ref, cols, scratch_cols, base, rows, masks):
    acc = jnp.broadcast_to(bias_ref[0:1, cols], (rows, HD))
    for k in range(TAPS):
        lag = TAPS - 1 - k
        window = xs[base - lag : base - lag + rows, scratch_cols]
        if lag:
            window = jnp.where(masks[lag], window, 0.0)
        acc = acc + taps_ref[k : k + 1, cols] * window
    return silu(acc).astype(BF16)


PACK = 640
PACKS = [(j, min(PACK, COLS + 256 - j)) for j in range(0, COLS + 256, PACK)]


def edge_kernel(
    doc_hbm, feat_hbm, proj_hbm, ftaps_hbm, fbias_hbm, ptaps_hbm, pbias_hbm, raw_hbm,
    sbias_hbm, dlog_hbm,
    out_ref, docv_ref, feat_ref, proj_ref, ftaps_ref, fbias_ref, ptaps_ref, pbias_ref, raw_ref,
    bias_ref, speed_ref, doc_ref, sbias_ref, dlog_ref, sems,
):
    tail = pl.ds(ROWS - 16, 16)
    bulk = pl.ds(0, ROWS - 16)
    copies = [
        pltpu.make_async_copy(source, target, sems.at[n])
        for n, (source, target) in enumerate((
            (feat_hbm.at[tail, :], feat_ref.at[tail, :]), (proj_hbm, proj_ref),
            (feat_hbm.at[bulk, :], feat_ref.at[bulk, :]), (doc_hbm, doc_ref),
            (ftaps_hbm, ftaps_ref), (fbias_hbm, fbias_ref), (ptaps_hbm, ptaps_ref),
            (pbias_hbm, pbias_ref), (raw_hbm, raw_ref), (sbias_hbm, sbias_ref),
            (dlog_hbm, dlog_ref),
        ))
    ]
    for copy in copies:
        copy.start()
    for copy in copies[:2]:
        copy.wait()
    last = jnp.concatenate(
        [feat_ref[ROWS - 16 :, :].astype(F32), proj_ref[ROWS - 16 :, :].astype(F32)], axis=1
    )
    last = last[16 - (TAPS - 1) :]
    rows = []
    for j, width in PACKS:
        piece = last[:, j : j + width]
        if width < PACK:
            piece = jnp.concatenate([piece, jnp.zeros((TAPS - 1, PACK - width), F32)], axis=1)
        rows.append(piece)
    rows.append(jnp.zeros((16 - (TAPS - 1) * len(PACKS), PACK), F32))
    out_ref[...] = jnp.concatenate(rows, axis=0).astype(BF16)
    for copy in copies[2:]:
        copy.wait()
    row = lax.broadcasted_iota(jnp.int32, (8, HD), 0)
    docv_ref[...] = jnp.where(row == 0, doc_ref[0], (ROWS - 1) - doc_ref[ROWS - 1])
    line = lax.broadcasted_iota(jnp.int32, (HEADS, HD), 0)
    bias = jnp.zeros((HEADS, HD), F32)
    speed = jnp.zeros((HEADS, HD), F32)
    for h in range(HEADS):
        bias = jnp.where(line == h, sbias_ref[h], bias)
        speed = jnp.where(line == h, dlog_ref[h], speed)
    bias_ref[...] = bias
    speed_ref[...] = speed


def split_decay(value):
    high = jnp.floor(value * 256.0) * (1.0 / 256.0)
    return jnp.concatenate([high, value - high], axis=0).astype(BF16)


def joined_decay(tile):
    wide = tile.astype(F32)
    half = tile.shape[0] // 2
    return wide[:half] + wide[half:]


def conv_kernel(
    docv_ref, feat_ref, proj_ref, ftaps_ref, fbias_ref, ptaps_ref, pbias_ref, raw_ref,
    sbias_ref, speed_ref,
    featc_ref, projc_ref, cum_ref, step_ref, coef_ref, decay_ref,
):
    first, start = docv_ref[0:1], docv_ref[1:2]
    first = jnp.concatenate([first, first], axis=1)
    start = jnp.concatenate([start, start], axis=1)
    t = lax.broadcasted_iota(jnp.int32, (ROWS, ROWS), 0)
    s = lax.broadcasted_iota(jnp.int32, (ROWS, ROWS), 1)
    offs = jnp.where((start > 0) & (t >= start), t - start, first + t)
    shifts = [
        jnp.where((t - s == lag) & (offs >= lag), 1.0, 0.0).astype(BF16) for lag in (1, 2, 3)
    ]

    def conv(x_ref, taps_ref, bias_ref, out_ref):
        for j in range(0, out_ref.shape[1], 256):
            cols = slice(j, j + 256)
            x = x_ref[:, cols]
            acc = jnp.broadcast_to(bias_ref[0:1, cols], (ROWS, 256))
            for k in range(TAPS):
                lag = TAPS - 1 - k
                if lag:
                    moved = jnp.dot(shifts[lag - 1], x, preferred_element_type=F32)
                else:
                    moved = x.astype(F32)
                acc = acc + taps_ref[k : k + 1, cols] * moved
            out_ref[:, cols] = silu(acc).astype(BF16)

    first, start = first[:, 0:1], start[:, 0:1]
    lane = lax.broadcasted_iota(jnp.int32, (HEADS, ROWS), 1)
    bias = sbias_ref[...]
    speed = jnp.exp(speed_ref[...])
    v = raw_ref[...] + jnp.concatenate([bias, bias], axis=1)
    step = jnp.maximum(v, 0.0) + jnp.log1p(jnp.exp(-jnp.abs(v)))
    cum = -step * jnp.concatenate([speed, speed], axis=1)
    shift = 1
    while shift < ROWS:
        cum = cum + jnp.where(lane >= shift, pltpu.roll(cum, shift, 1), 0.0)
        shift *= 2
    conv(proj_ref, ptaps_ref, pbias_ref, projc_ref)
    conv(feat_ref, ftaps_ref, fbias_ref, featc_ref)
    last = cum[:, ROWS - 1 : ROWS]
    cum_ref[...] = cum
    step_ref[...] = step
    tail = (start <= 0) | (lane >= start)
    coef_ref[...] = jnp.where(tail, jnp.exp(last - cum) * step, 0.0)
    kept = (docv_ref[1:2] < 0) & (docv_ref[0:1] >= 1)
    decay_ref[...] = jnp.where(kept, jnp.broadcast_to(jnp.exp(last), (HEADS, HD)), 0.0)


def state_kernel(
    docv_ref, rim_ref, feat_ref, proj_ref, ftaps_ref, fbias_ref, ptaps_ref, pbias_ref,
    coef_ref, decay_ref, featc_in, projc_in,
    featc_ref, projc_ref, keep_ref, send_ref, rest_ref, xs,
):
    del featc_in, projc_in
    rim = rim_ref[...].astype(F32)
    for n, (j, width) in enumerate(PACKS):
        xs[16 - (TAPS - 1) : 16, j : j + width] = rim[
            n * (TAPS - 1) : (n + 1) * (TAPS - 1), :width
        ]
    xs[16:32, :COLS] = feat_ref[0:16, :].astype(F32)
    xs[16:32, COLS:] = proj_ref[0:16, :].astype(F32)
    first, start = docv_ref[0:1], docv_ref[1:2]
    t = lax.broadcasted_iota(jnp.int32, (16, HD), 0)
    offs = jnp.where((start > 0) & (t >= start), t - start, first + t)
    masks = {lag: offs >= lag for lag in (1, 2, 3)}
    for j in range(2):
        cols = slice(j * HD, (j + 1) * HD)
        there = slice(COLS + j * HD, COLS + (j + 1) * HD)
        projc_ref[0:16, cols] = conv_rows(xs, ptaps_ref, pbias_ref, cols, there, 16, 16, masks)
    for j in range(HEADS):
        cols = slice(j * HD, (j + 1) * HD)
        featc_ref[0:16, cols] = conv_rows(xs, ftaps_ref, fbias_ref, cols, cols, 16, 16, masks)
    turned = projc_ref[:, :HD].astype(F32).T
    for n, h in enumerate(order_of(1 - my_core())):
        rows = pl.ds(pl.multiple_of(h * HD, HD), HD)
        scaled = (turned * coef_ref[pl.ds(h, 1), :]).astype(BF16)
        added = jnp.dot(scaled, featc_ref[:, rows], preferred_element_type=F32)
        keep_ref[rows, :] = added
        if n < SOON:
            send_ref[n * HD : (n + 1) * HD, :] = added.astype(BF16)
        else:
            rest_ref[(n - SOON) * HD : (n - SOON + 1) * HD, :] = added.astype(BF16)
    send_ref[SOON * HD :, :] = split_decay(decay_ref[...])


def chip_kernel(keep_ref, decay_ref, recv_ref, own_ref, own_decay_ref, a_ref, b_ref, decays):
    core = my_core()
    second = core == 1
    k = my_slice()
    theirs = joined_decay(recv_ref[SOON * HD :, :])
    mine = decay_ref[...]
    decays[0:16, :] = jnp.where(second, mine, theirs)
    decays[16:32, :] = mine * theirs
    decays[32:40, :] = jnp.zeros((8, HD), F32)

    order = order_of(core)

    def combined(n):
        h = order[n]
        a = keep_ref[pl.ds(pl.multiple_of(h * HD, HD), HD), :]
        b = recv_ref[n * HD : (n + 1) * HD, :].astype(F32)
        return decays[pl.ds(h, 1), :] * jnp.where(second, b, a) + jnp.where(second, a, b)

    for i in range(4):
        a_ref[i * HD : (i + 1) * HD, :] = combined(4 + i).astype(BF16)
    a_ref[4 * HD :, :] = split_decay(decays[pl.ds(16 + order[4], 8), :])
    for i in range(2):
        b_ref[i * HD : (i + 1) * HD, :] = combined(8 + i).astype(BF16)
    b_ref[2 * HD :, :] = split_decay(decays[pl.ds(16 + 4 * lax.bitwise_xor(k, 2), 8), :])
    for i in range(4):
        own_ref[i * HD : (i + 1) * HD, :] = combined(i)
    own_decay_ref[...] = decays[pl.ds(16 + 4 * k, 8), :]


QUARTER = 4 * HD


def half_rows(core):
    return pl.ds(pl.multiple_of(core * 2 * HD, 2 * HD), 2 * HD)


def group_kernel(
    own_ref, own_decay_ref, ra_ref, ga_ref, rb_ref, gb_ref,
    total_ref, chips_ref, decays_ref,
):
    core = my_core()
    spot = my_spot()
    chips_ref[spot] = own_ref[...]
    decays_ref[spot] = own_decay_ref[...]
    for ref, m in ((ra_ref, 1 + 2 * core), (ga_ref, 3 - 2 * core)):
        there = lax.bitwise_xor(spot, m)
        chips_ref[there] = ref[:QUARTER, :].astype(F32)
        decays_ref[there] = joined_decay(ref[QUARTER:, :])
    there = lax.bitwise_xor(spot, 2)
    chips_ref[there, half_rows(core), :] = rb_ref[: 2 * HD, :].astype(F32)
    chips_ref[there, half_rows(1 - core), :] = gb_ref[: 2 * HD, :].astype(F32)
    decays_ref[there] = joined_decay(rb_ref[2 * HD :, :])
    for i in range(4):
        rows = slice(i * HD, (i + 1) * HD)
        total = chips_ref[0, rows, :]
        for q in range(1, 4):
            total = decays_ref[q, i : i + 1, :] * total + chips_ref[q, rows, :]
        total_ref[rows, :] = total.astype(BF16)
    total_ref[QUARTER:, :] = split_decay(
        decays_ref[0] * decays_ref[1] * decays_ref[2] * decays_ref[3]
    )


def enter_kernel(chips_ref, decays_ref, q_ref, other_ref, own_ref, a_ref, b_ref, states):
    core = my_core()
    second = core == 1
    spot = my_spot()
    q = q_ref[...].astype(F32)
    other = other_ref[...].astype(F32)
    before = jnp.where(second, other, q)
    farther = jnp.where(second, q, other)
    decay = joined_decay(before[QUARTER:])
    group = lax.div(lax.axis_index("ctx"), 8)
    before = jnp.where(group >= 1, before, 0.0)
    farther = jnp.where(group >= 2, farther, 0.0)
    for i in range(4):
        rows = slice(i * HD, (i + 1) * HD)
        state = before[rows] + decay[i : i + 1] * farther[rows]
        for n in range(4):
            states[n, rows, :] = state
            if n < 3:
                state = decays_ref[n, i : i + 1, :] * state + chips_ref[n, rows, :]
    a_ref[...] = states[lax.bitwise_xor(spot, 1 + 2 * core)].astype(BF16)
    b_ref[...] = states[lax.bitwise_xor(spot, 2), half_rows(core), :].astype(BF16)
    own_ref[...] = states[spot]


def inner_kernel(
    docv_ref, featc_ref, projc_ref, cum_ref, step_ref, gate_hbm, skip_hbm, gain_hbm,
    a_ref, g_ref, gain_ref, masked, gate_ref, skip_ref, sems,
):
    copies = [
        pltpu.make_async_copy(gate_hbm, gate_ref, sems.at[0]),
        pltpu.make_async_copy(skip_hbm, skip_ref, sems.at[1]),
        pltpu.make_async_copy(gain_hbm, gain_ref, sems.at[2]),
    ]
    for copy in copies:
        copy.start()
    first, start = docv_ref[0:1], docv_ref[1:2]
    scores = lax.dot_general(
        projc_ref[:, HD:], projc_ref[:, :HD], (((1,), (1,)), ((), ())),
        preferred_element_type=F32,
    )
    t = lax.broadcasted_iota(jnp.int32, (ROWS, ROWS), 0)
    s = lax.broadcasted_iota(jnp.int32, (ROWS, ROWS), 1)
    wide_start = jnp.concatenate([start, start], axis=1)
    same = (s <= t) & ((s >= wide_start) | (t < wide_start))
    masked[...] = jnp.where(same, scores, 0.0)
    cum = cum_ref[...] * LOG2E
    row_side = cum - jnp.log(step_ref[...]) * LOG2E
    padded = jnp.concatenate([cum, jnp.zeros((HD - HEADS, ROWS), F32)], axis=0)
    columns = padded.T
    t_col = lax.broadcasted_iota(jnp.int32, (ROWS, HD), 0)
    reach = (first >= 1) & ((t_col < start) | (start <= 0))
    for copy in copies:
        copy.wait()
    for h in range(HEADS):
        cols = slice(h * HD, (h + 1) * HD)
        column = jnp.broadcast_to(columns[:, h : h + 1], (ROWS, HD))
        lift = jnp.where(reach, jnp.exp2(column), 0.0)
        gate = silu(gate_ref[:, cols].astype(F32))
        g_ref[h] = gate * lift
        for top in (0, HD):
            width = top + HD
            tall = column[top : top + HD]
            wide = jnp.concatenate([tall] * (width // HD), axis=1)
            gap = jnp.minimum(wide - row_side[h : h + 1, :width], 60.0)
            weights = (masked[top : top + HD, :width] * jnp.exp2(gap)).astype(BF16)
            inner = jnp.dot(weights, featc_ref[:width, cols], preferred_element_type=F32)
            feat = featc_ref[top : top + HD, cols].astype(F32)
            a_ref[h, top : top + HD, :] = (inner + skip_ref[h] * feat) * gate[top : top + HD]


def lifted_heads(refs, heads, early_ref, decays, c, a_ref, g_ref, gain_ref, gated_ref, total):
    second = my_core() == 1
    states = [
        ref[i * HD : (i + 1) * HD, :] for ref in refs for i in range(ref.shape[0] // HD)
    ]
    for n, (h, state) in enumerate(zip(heads, states, strict=True)):
        state = state.astype(F32)
        early = early_ref[n * HD : (n + 1) * HD, :].astype(F32)
        state = jnp.where(second, decays[pl.ds(h, 1), :] * state + early, state)
        high = state.astype(BF16)
        low = (state - high.astype(F32)).astype(BF16)
        lifted = jnp.dot(c, high, preferred_element_type=F32) + jnp.dot(
            c, low, preferred_element_type=F32
        )
        gated = a_ref[h] + lifted * g_ref[h]
        cols = pl.ds(pl.multiple_of(h * HD, HD), HD)
        gated_ref[h] = gated * gain_ref[0:1, cols]
        total = total + gated * gated
    return total


def gated_kernel(
    projc_ref, recv_ref, own_ref, fa_ref, fb_ref, a_ref, g_ref, gain_ref,
    gated_ref, total_ref, decays_ref,
):
    decays_ref[...] = joined_decay(recv_ref[SOON * HD :, :])
    total_ref[...] = lifted_heads(
        (own_ref, fa_ref, fb_ref), order_of(my_core())[:SOON], recv_ref, decays_ref,
        projc_ref[:, HD:], a_ref, g_ref, gain_ref, gated_ref, jnp.zeros((ROWS, HD), F32),
    )


def last_gated_kernel(
    projc_ref, rest_ref, decays_ref, ha_ref, hb_ref, a_ref, g_ref, gain_ref, gated_in, total_ref,
    gated_ref, squares_ref,
):
    del gated_in
    total = lifted_heads(
        (ha_ref, hb_ref), order_of(my_core())[SOON:], rest_ref, decays_ref,
        projc_ref[:, HD:], a_ref, g_ref, gain_ref, gated_ref, total_ref[...],
    )
    squares_ref[...] = jnp.broadcast_to(
        jnp.sum(total.T, axis=0, keepdims=True), (8, ROWS)
    )


def norm_kernel(gated_ref, s0, s1, s3, s2, out_hbm, out_ref, sems):
    total = (s0[0:1] + s1[0:1]) + (s2[0:1] + s3[0:1])
    scale = lax.rsqrt(total / (COLS * YS) + 1e-05)
    scale = jnp.broadcast_to(scale, (HD, ROWS)).T
    copies = []
    for i in range(HEADS):
        cols = slice(i * HD, (i + 1) * HD)
        out_ref[:, cols] = (gated_ref[i] * scale).astype(BF16)
        if i % 2 == 1:
            cols = pl.ds((i - 1) * HD, 2 * HD)
            copy = pltpu.make_async_copy(
                out_ref.at[:, cols], out_hbm.at[:, cols], sems.at[i // 2]
            )
            copy.start()
            copies.append(copy)
    for copy in copies:
        copy.wait()


VMEM = pl.BlockSpec(memory_space=pltpu.VMEM)
HBM = pl.BlockSpec(memory_space=pl.ANY)
DMA = pltpu.SemaphoreType.DMA


def shaped(*shape, dtype=BF16):
    return jax.ShapeDtypeStruct(shape, dtype)


def call(kernel, name, out, args, far=(), scratch=(), aliases=None, out_specs=None):
    single = not isinstance(out, (list, tuple))
    args = [
        pltpu.with_memory_space_constraint(x, pltpu.HBM) if i in far else x
        for i, x in enumerate(args)
    ]
    return pl.pallas_call(
        kernel,
        name=name,
        out_shape=out,
        in_specs=[HBM if i in far else VMEM for i in range(len(args))],
        out_specs=out_specs or (VMEM if single else [VMEM] * len(out)),
        scratch_shapes=list(scratch),
        input_output_aliases=aliases or {},
        compiler_params=pltpu.CompilerParams(vmem_limit_bytes=VMEM_LIMIT),
    )(*args)


def body(
    feat_in, gate_in, state_proj, step_raw, doc_offset, feat_taps, feat_bias,
    proj_taps, proj_bias, step_bias, decay_log, skip_gain, norm_gain,
):
    fbias = feat_bias.reshape(1, COLS)
    pbias = proj_bias.reshape(1, 256)
    gain = norm_gain.reshape(1, COLS)
    f32 = functools.partial(shaped, dtype=F32)

    params = [f32(TAPS, COLS), f32(1, COLS), f32(TAPS, 256), f32(1, 256)]
    edge, docv, feat, proj, *params, raw, bias, speed = call(
        edge_kernel, "edge",
        [
            shaped(16, PACK), shaped(8, HD, dtype=jnp.int32), shaped(ROWS, COLS),
            shaped(ROWS, 256), *params, f32(HEADS, ROWS), f32(HEADS, HD), f32(HEADS, HD),
        ],
        (
            doc_offset, feat_in, state_proj, feat_taps, fbias, proj_taps, pbias, step_raw,
            step_bias, decay_log,
        ),
        far=range(10),
        scratch=[
            pltpu.SMEM((ROWS,), jnp.int32), pltpu.SMEM((HEADS,), F32),
            pltpu.SMEM((HEADS,), F32), DMA((11,)),
        ],
    )
    rim = lax.ppermute(edge, "ctx", NEXT)

    featc, projc, cum, step, coef, decay = call(
        conv_kernel, "conv",
        [
            shaped(ROWS, COLS), shaped(ROWS, 256), f32(HEADS, ROWS), f32(HEADS, ROWS),
            f32(HEADS, ROWS), f32(HEADS, HD),
        ],
        (docv, feat, proj, *params, raw, bias, speed),
    )
    featc, projc, keep, send, rest = call(
        state_kernel, "state",
        [
            shaped(ROWS, COLS), shaped(ROWS, 256), f32(COLS, HD), shaped(SOON * HD + 32, HD),
            shaped((HEADS - SOON) * HD, HD),
        ],
        (docv, rim, feat, proj, *params, coef, decay, featc, projc),
        scratch=[pltpu.VMEM((32, COLS + 256), F32)],
        aliases={10: 0, 11: 1},
    )
    recv = lax.ppermute(send, "ctx", CORE)

    own, own_decay, ta, tb = call(
        chip_kernel, "chip",
        [f32(QUARTER, HD), f32(8, HD), shaped(QUARTER + 16, HD), shaped(2 * HD + 16, HD)],
        (keep, decay, recv),
        scratch=[pltpu.VMEM((40, HD), F32)],
    )
    rb = lax.ppermute(tb, "ctx", TWO)
    ra = lax.ppermute(ta, "ctx", APART)
    featc, projc, ta = lax.optimization_barrier((featc, projc, ta))
    a, g, gain = call(
        inner_kernel, "inner",
        [f32(HEADS, ROWS, HD), f32(HEADS, ROWS, HD), f32(1, COLS)],
        (docv, featc, projc, cum, step, gate_in, skip_gain, gain),
        far=(5, 6, 7),
        scratch=[
            pltpu.VMEM((ROWS, ROWS), F32),
            pltpu.VMEM((ROWS, COLS), BF16),
            pltpu.SMEM((HEADS,), F32),
            DMA((3,)),
        ],
    )
    ra, a = lax.optimization_barrier((ra, a))
    ga = lax.ppermute(ra, "ctx", CORE)
    gb = lax.ppermute(rb, "ctx", CORE)
    total, chips, decays = call(
        group_kernel, "group",
        [shaped(QUARTER + 16, HD), f32(4, QUARTER, HD), f32(4, 8, HD)],
        (own, own_decay, ra, ga, rb, gb),
    )
    q = lax.ppermute(total, "ctx", LATER)
    rest, chips = lax.optimization_barrier((rest, chips))
    rest = lax.ppermute(rest, "ctx", CORE)
    other = lax.ppermute(q, "ctx", CORE)
    other, rest = lax.optimization_barrier((other, rest))
    e_own, ea, eb = call(
        enter_kernel, "enter",
        [f32(QUARTER, HD), shaped(QUARTER, HD), shaped(2 * HD, HD)],
        (chips, decays, q, other),
        scratch=[pltpu.VMEM((4, QUARTER, HD), F32)],
    )
    fb = lax.ppermute(eb, "ctx", TWO)
    fa = lax.ppermute(ea, "ctx", APART)
    ha = lax.ppermute(fa, "ctx", CORE)
    hb = lax.ppermute(fb, "ctx", CORE)
    gated, squares, early_decay = call(
        gated_kernel, "gated", [f32(HEADS, ROWS, HD), f32(ROWS, HD), f32(HEADS, HD)],
        (projc, recv, e_own, fa, fb, a, g, gain),
    )
    gated, squares = call(
        last_gated_kernel, "last_gated", [f32(HEADS, ROWS, HD), f32(8, ROWS)],
        (projc, rest, early_decay, ha, hb, a, g, gain, gated, squares),
        aliases={8: 0},
    )
    s2 = lax.ppermute(squares, "head", HEAD_XOR[2])
    s3 = lax.ppermute(squares, "head", HEAD_XOR[3])
    s1 = lax.ppermute(squares, "head", HEAD_XOR[1])
    return call(
        norm_kernel, "norm", shaped(ROWS, COLS), (gated, squares, s1, s3, s2),
        scratch=[pltpu.VMEM((ROWS, COLS), BF16), DMA((HEADS // 2,))],
        out_specs=HBM,
    )


def solution(mesh):
    return jax.shard_map(
        body,
        mesh=mesh,
        in_specs=(
            P("ctx", "head"),
            P("ctx", "head"),
            P("ctx", None),
            P("head", "ctx"),
            P("ctx"),
            P(None, "head"),
            P("head"),
            P(),
            P(),
            P("head"),
            P("head"),
            P("head"),
            P("head"),
        ),
        out_specs=P("ctx", "head"),
        check_vma=False,
    )
```
